32 devices in a mesh: fsdp: 4 (over x, core), ctx: 8 (over z, y).
Axes of the slice: x: 2, y: 2, z: 4, core: 2. Of those that a mesh axis runs over, the one named last changes fastest.
Arguments:
- hidden: bfloat16 [4, 1024, 2304], P('fsdp', 'ctx'), may hold values from -6 to 6
- query_heads: bfloat16 [4, 1024, 2048], P('fsdp', 'ctx'), may hold values from -6 to 6
- key_heads: bfloat16 [4, 1024, 2048], P('fsdp', 'ctx'), may hold values from -6 to 6
- value_heads: bfloat16 [4, 1024, 2048], P('fsdp', 'ctx'), may hold values from -6 to 6
- out_grad: bfloat16 [4, 1024, 2048], P('fsdp', 'ctx'), may hold values from -6 to 6
- checkpoint: float32 [4, 8, 16, 128, 128], P('fsdp', 'ctx'), may hold values from -6 to 6
- gate_down: bfloat16 [2304, 128], P('fsdp'), may hold values from -0.125 to 0.125
- gate_up: bfloat16 [128, 2048], P(None, 'fsdp'), may hold values from -0.5 to 0.5
- gate_bias: float32 [2048], replicated, may hold values from -4 to 4
- decay_rate: float32 [2048], replicated, may hold values from 0.0001953125 to 0.05
- beta_weight: bfloat16 [2304, 16], P('fsdp'), may hold values from -0.125 to 0.125
Outputs:
- query_grad: bfloat16 [4, 1024, 2048], P('fsdp', 'ctx')
- key_grad: bfloat16 [4, 1024, 2048], P('fsdp', 'ctx')
- value_grad: bfloat16 [4, 1024, 2048], P('fsdp', 'ctx')
- hidden_grad: bfloat16 [4, 1024, 2304], P('fsdp', 'ctx')
- gate_down_grad: float32 [2304, 128], P('fsdp')
- gate_up_grad: float32 [128, 2048], P(None, 'fsdp')
- beta_weight_grad: float32 [2304, 16], P('fsdp')
- gate_bias_grad: float32 [2048], replicated
- decay_rate_grad: float32 [2048], replicated
The draws below stay inside these ranges and needn't reach their ends.
All inputs are finite; a program needn't handle non-finite values.
Results may differ from the reference program's by a relative error of at most 0.0052.
Values may be sent and summed in bfloat16 or wider, within the bound.
A program may use at most 256 MiB of HBM per device.

```python
import math
import jax
import jax.numpy as jnp
from jax import lax

D = 2304
HEADS = 16
HEAD = 128
RANK = 128
CH = 128
TOK_DEV = 128
LENGTH = 1024
SEQS = 4
N_CTX = 8


def shard_levels(own_key, dims, cuts, least, largest):
    level, own = 1.0, jax.random.fold_in(own_key, 6)
    for dim, blocks in cuts:
        heights = jnp.exp(jax.random.uniform(jax.random.fold_in(own, dim), (blocks,), jnp.float32, least / len(cuts), largest / len(cuts)))
        level = level * jnp.repeat(heights, dims[dim] // blocks).reshape([-1 if axis == dim else 1 for axis in range(len(dims))])
    return level


def centred(rng, extent, spread, reach, shards=(), kind=jnp.bfloat16):
    loudness = shard_levels(rng, extent, shards, -0.22, 0.18) if shards else 1.0
    result = jax.random.normal(rng, extent, jnp.float32) * spread * loudness
    return jnp.minimum(jnp.maximum(result, -reach), reach).astype(kind)


def setup_inputs(seed: int = 0) -> dict:
    streams_of = jax.random.split(jax.random.key(seed), 12)
    return {
        "hidden": centred(streams_of[0], (SEQS, LENGTH, D), 1.0, 6.0, ((0, 4), (1, 8))),
        "query_heads": centred(streams_of[1], (SEQS, LENGTH, HEADS * HEAD), 1.0, 6.0, ((0, 4), (1, 8))),
        "key_heads": centred(streams_of[2], (SEQS, LENGTH, HEADS * HEAD), 1.0, 6.0, ((0, 4), (1, 8))),
        "value_heads": centred(streams_of[3], (SEQS, LENGTH, HEADS * HEAD), 1.0, 6.0, ((0, 4), (1, 8))),
        "out_grad": centred(streams_of[4], (SEQS, LENGTH, HEADS * HEAD), 1.0, 6.0, ((0, 4), (1, 8))),
        "checkpoint": centred(streams_of[5], (SEQS, N_CTX, HEADS, HEAD, HEAD), 1.0, 6.0, ((0, 4), (1, 8)), jnp.float32),
        "gate_down": centred(streams_of[6], (D, RANK), D ** -0.5, 0.125, ((0, 4),)),
        "gate_up": centred(streams_of[7], (RANK, HEADS * HEAD), RANK ** -0.5, 0.5, ((1, 4),)),
        "gate_bias": centred(streams_of[8], (HEADS * HEAD,), 1.0, 4.0, (), jnp.float32),
        "decay_rate": jnp.clip(jnp.exp(jax.random.uniform(streams_of[9], (HEADS * HEAD,), jnp.float32, math.log(0.0001953125), math.log(0.05))), 0.0001953125, 0.05),
        "beta_weight": centred(streams_of[10], (D, HEADS), D ** -0.5, 0.125, ((0, 4),)),
    }


PRECISE = lax.Precision.HIGHEST
EPSILON = 1e-06

def unit_rows(matrix):
    return matrix * lax.rsqrt(lax.optimization_barrier(jnp.sum(matrix * matrix, axis=-1, keepdims=True)) + EPSILON)

def to_spans(values):
    tok_rows = values.shape[0]
    return values.reshape((tok_rows // CH, CH) + values.shape[1:]).swapaxes(1, 2)

def tri_masks():
    row_index = lax.broadcasted_iota(jnp.int32, (CH, CH), 0)
    col_index = lax.broadcasted_iota(jnp.int32, (CH, CH), 1)
    return ((row_index > col_index).astype(jnp.float32), (row_index >= col_index).astype(jnp.float32))

def span_terms(k_span, g_span, b_span):
    cumulative = jnp.cumsum(g_span, axis=1)
    key_plus = k_span * jnp.exp(cumulative)
    key_minus = k_span * jnp.exp(-cumulative)
    key_end = k_span * jnp.exp(cumulative[:, -1:, :] - cumulative)
    strict, _ = tri_masks()
    mixing = jnp.einsum('htc,hsc->hts', key_plus, key_minus, precision=PRECISE) * strict * b_span[:, :, None]
    system = mixing + jnp.eye(CH, dtype=jnp.float32)
    return (cumulative, key_plus, key_minus, key_end, system)

def block_forward(start_state, queries, keys_in, values_in, decay_heads, beta_gate):
    q_all = to_spans(unit_rows(queries))
    k_all = to_spans(unit_rows(keys_in))
    v_all = to_spans(values_in)
    g_all = to_spans(decay_heads)
    b_all = to_spans(beta_gate)
    _, inclusive = tri_masks()

    def advance(carried, pieces):
        q_span, k_span, v_span, g_span, b_span = pieces
        cumulative, key_plus, key_minus, key_end, system = span_terms(k_span, g_span, b_span)
        query_plus = q_span * jnp.exp(cumulative)
        target = b_span[:, :, None] * (v_span - jnp.einsum('htc,hcd->htd', key_plus, carried, precision=PRECISE))
        updates = jax.scipy.linalg.solve_triangular(system, target, lower=True, unit_diagonal=True)
        scores = jnp.einsum('htc,hsc->hts', query_plus, key_minus, precision=PRECISE) * inclusive
        outputs = jnp.einsum('htc,hcd->htd', query_plus, carried, precision=PRECISE) + jnp.einsum('hts,hsd->htd', scores, updates, precision=PRECISE)
        renewed = jnp.exp(cumulative[:, -1, :])[:, :, None] * carried + jnp.einsum('hsc,hsd->hcd', key_end, updates, precision=PRECISE)
        return (renewed, outputs)
    end_state, outputs = lax.scan(advance, start_state, (q_all, k_all, v_all, g_all, b_all))
    return (outputs.swapaxes(1, 2).reshape(queries.shape), end_state)

def gate_forward(hidden_rows, down_full, up_full, gate_bias, decay_rate, beta_full):
    low_rank = jnp.dot(hidden_rows.astype(jnp.float32), down_full.astype(jnp.float32), preferred_element_type=jnp.float32).astype(jnp.bfloat16)
    gate_input = jnp.dot(low_rank.astype(jnp.float32), up_full.astype(jnp.float32), preferred_element_type=jnp.float32) + gate_bias
    log_decay = -decay_rate * jax.nn.softplus(gate_input)
    beta_gate = jax.nn.sigmoid(jnp.dot(hidden_rows.astype(jnp.float32), beta_full.astype(jnp.float32), preferred_element_type=jnp.float32))
    return (low_rank, gate_input, log_decay, beta_gate)

def contract_rows(left, right):
    return lax.dot_general(left.astype(jnp.float32), right.astype(jnp.float32), (((0,), (0,)), ((), ())), preferred_element_type=jnp.float32)

def contract_cols(left, right):
    return lax.dot_general(left.astype(jnp.float32), right.astype(jnp.float32), (((1,), (1,)), ((), ())), preferred_element_type=jnp.float32)

def gate_backward(hidden_rows, low_rank, gate_input, beta_gate, decay_cot, beta_cot, down_full, up_full, decay_rate, beta_full):
    input_grad = decay_cot * -decay_rate * jax.nn.sigmoid(gate_input)
    input_half = input_grad.astype(jnp.bfloat16)
    rate_term = -lax.optimization_barrier(jnp.sum(decay_cot * jax.nn.softplus(gate_input), axis=0))
    bias_term = lax.optimization_barrier(jnp.sum(input_grad, axis=0))
    up_term = contract_rows(low_rank, input_half)
    low_grad = contract_cols(input_half, up_full).astype(jnp.bfloat16)
    score_grad = (beta_cot * beta_gate * (1.0 - beta_gate)).astype(jnp.bfloat16)
    down_term = contract_rows(hidden_rows, low_grad)
    beta_term = contract_rows(hidden_rows, score_grad)
    hidden_grad = (contract_cols(low_grad, down_full) + contract_cols(score_grad, beta_full)).astype(jnp.bfloat16)
    return (hidden_grad, down_term, up_term, beta_term, bias_term, rate_term)

def reference(hidden, query_heads, key_heads, value_heads, out_grad, checkpoint, gate_down, gate_up, gate_bias, decay_rate, beta_weight):
    seq_count, seq_length, model_width = hidden.shape
    count_heads, size_head = (checkpoint.shape[2], checkpoint.shape[3])
    hidden_rows = hidden.reshape(seq_count * seq_length, model_width)
    low_rank, gate_input, log_decay, beta_gate = gate_forward(hidden_rows, gate_down, gate_up, gate_bias, decay_rate, beta_weight)

    def blocked(values, trailing):
        return values.reshape((seq_count, N_CTX, TOK_DEV) + trailing).swapaxes(0, 1)
    full_heads = (count_heads, size_head)

    def one_block(start_state, queries, keys_in, values_in, decay_block, beta_block, grad_block, end_grad):
        _, pullback = jax.vjp(block_forward, start_state, queries.astype(jnp.float32), keys_in.astype(jnp.float32), values_in.astype(jnp.float32), decay_block, beta_block)
        start_grad, q_grad, k_grad, v_grad, d_grad, b_grad = pullback((grad_block.astype(jnp.float32), end_grad))
        return (start_grad, q_grad.astype(jnp.bfloat16), k_grad.astype(jnp.bfloat16), v_grad.astype(jnp.bfloat16), d_grad, b_grad)
    batched = jax.vmap(one_block)

    def backward_step(end_grad, pieces):
        results = batched(pieces[0], pieces[1], pieces[2], pieces[3], pieces[4], pieces[5], pieces[6], end_grad)
        return (results[0], results[1:])
    pieces = (checkpoint.swapaxes(0, 1), blocked(query_heads, full_heads), blocked(key_heads, full_heads), blocked(value_heads, full_heads), blocked(log_decay, full_heads), blocked(beta_gate, (count_heads,)), blocked(out_grad, full_heads))
    zero_grad = jnp.zeros((seq_count, count_heads, size_head, size_head), jnp.float32)
    _, stacked = lax.scan(backward_step, zero_grad, pieces, reverse=True)

    def unblock(values):
        return values.swapaxes(0, 1).reshape(seq_count, seq_length, -1)
    query_grad = unblock(stacked[0])
    key_grad = unblock(stacked[1])
    value_grad = unblock(stacked[2])
    decay_cot = unblock(stacked[3]).reshape(seq_count * seq_length, -1)
    beta_cot = unblock(stacked[4]).reshape(seq_count * seq_length, -1)
    hidden_grad, down_term, up_term, beta_term, bias_term, rate_term = gate_backward(hidden_rows, low_rank, gate_input, beta_gate, decay_cot, beta_cot, gate_down, gate_up, decay_rate, beta_weight)
    return (query_grad, key_grad, value_grad, hidden_grad.reshape(seq_count, seq_length, model_width), down_term, up_term, beta_term, bias_term, rate_term)
```

```python
import functools

import jax
import jax.numpy as jnp
from jax import lax
from jax.experimental import pallas as pl
from jax.experimental.pallas import tpu as pltpu
from jax.sharding import PartitionSpec as P

EPSILON = 1e-06
MESH = pl.DeviceIdType.MESH
F32, BF16 = jnp.float32, jnp.bfloat16
VMEM_LIMIT = 48 * 1024 * 1024
NN, NT, TN = ((1,), (0,)), ((1,), (1,)), ((0,), (0,))
INV_PASSES = 1
PASSES = 3


def dot(left, right, dims=NN):
    return lax.dot_general(left, right, (dims, ((), ())), preferred_element_type=F32)


def halves(value):
    if value.dtype == BF16:
        return value, None
    high = value.astype(BF16)
    return high, (value - high.astype(F32)).astype(BF16)


def mm(left, right, dims=NN, passes=None):
    passes = PASSES if passes is None else passes
    if passes == 1:
        return dot(left.astype(BF16), right.astype(BF16), dims)
    left_high, left_low = halves(left)
    right_high, right_low = halves(right)
    total = dot(left_high, right_high, dims)
    if left_low is not None:
        total += dot(left_low, right_high, dims)
    if right_low is not None:
        total += dot(left_high, right_low, dims)
    return total


def sum_by(ones, value):
    high = value.astype(BF16)
    rest = value - high.astype(F32)
    mid = rest.astype(BF16)
    low = (rest - mid.astype(F32)).astype(BF16)
    return dot(ones, high) + dot(ones, mid) + dot(ones, low)


def iotas(size):
    return (
        lax.broadcasted_iota(jnp.int32, (size, size), 0),
        lax.broadcasted_iota(jnp.int32, (size, size), 1),
    )


def inverse(systems):
    size = systems[0].shape[0]
    row, col = iotas(size)
    eye = jnp.where(row == col, 1.0, 0.0)

    def off(block):
        same = row // (2 * block) == col // (2 * block)
        return same & ((row // block) % 2 == 1) & ((col // block) % 2 == 0)

    found = [eye - jnp.where(off(1), system, 0.0) for system in systems]
    block = 2
    while block < size:
        mask = off(block)
        parts = [mm(jnp.where(mask, s, 0.0), t, NN, INV_PASSES) for s, t in zip(systems, found)]
        found = [t - mm(t, p, NN, INV_PASSES) for t, p in zip(found, parts)]
        block *= 2
    return found


def softplus(value):
    return jnp.maximum(value, 0.0) + jnp.log1p(jnp.exp(-jnp.abs(value)))


def sigmoid(value):
    return 1.0 / (1.0 + jnp.exp(-value))


def unit(rows):
    scale = lax.rsqrt(jnp.sum(rows * rows, axis=-1, keepdims=True) + EPSILON)
    return rows * scale, scale


def unit_back(grad, rows, scale):
    return scale * (grad - rows * jnp.sum(grad * rows, axis=-1, keepdims=True))


def head_terms(keys, gate_in, rate):
    size = keys.shape[0]
    row, col = iotas(size)
    kn, k_scale = unit(keys.astype(F32))
    ones = jnp.where(row >= col, 1.0, 0.0).astype(BF16)
    cumulative = sum_by(ones, -rate * softplus(gate_in))
    return kn, k_scale, cumulative


def local_heads(heads):
    row, col = iotas(heads[0]["k"].shape[0])
    for h in heads:
        kn, _, cum = head_terms(h["k"], h["gate_in"], h["rate"])
        qn, q_scale = unit(h["q"].astype(F32))
        plus = jnp.exp(cum)
        h.update(cum=cum, qn=qn, q_scale=q_scale, plus=plus)
        h.update(kp=kn * plus, km=kn * jnp.exp(-cum), qp=qn * plus)
        h.update(ke=kn * jnp.exp(cum[-1:] - cum), gf=h["go"].astype(F32))
    for h in heads:
        h["kk"] = jnp.where(row > col, mm(h["kp"], h["km"], NT), 0.0)
        h["p"] = jnp.where(row >= col, mm(h["qp"], h["km"], NT), 0.0)
    for h, t in zip(heads, inverse([h["kk"] * h["beta"] for h in heads])):
        h["t"] = t
    for h in heads:
        h["r"] = h["v"].astype(F32) - mm(h["kp"], h["s"])
        h["pg"] = mm(h["p"], h["go"], TN)
    for h in heads:
        h["u"] = mm(h["t"], h["beta"] * h["r"])
        h["wa"] = mm(h["t"], h["ke"], TN)
        h["wb"] = mm(h["t"], h["pg"], TN)
    for h in heads:
        kb = h["kp"] * h["beta"]
        end = jnp.exp(h["cum"][-1:])
        h["map"] = jnp.where(row == col, end, 0.0) - mm(kb, h["wa"], TN)
        h["add"] = mm(h["qp"], h["go"], TN) - mm(kb, h["wb"], TN)
        h["dp"] = jnp.where(row >= col, mm(h["go"], h["u"], NT), 0.0)
    for h in heads:
        dqp = mm(h["go"], h["s"], NT) + mm(h["dp"], h["km"])
        h["dq"] = unit_back(dqp * h["plus"], h["qn"], h["q_scale"])
        h["dcum"] = dqp * h["qp"]
        h["dkm"] = mm(h["dp"], h["qp"], TN)
    return heads


def back_heads(heads):
    size = heads[0]["k"].shape[0]
    row, col = iotas(size)
    ones = jnp.where(row <= col, 1.0, 0.0).astype(BF16)
    for h in heads:
        kn, k_scale = unit(h["k"].astype(F32))
        cum = h["cum"]
        plus, minus, end = jnp.exp(cum), jnp.exp(-cum), jnp.exp(cum[-1:] - cum)
        h.update(kn=kn, k_scale=k_scale, plus=plus, minus=minus, end=end, kp=kn * plus)
        h["w"] = h["wb"] + mm(h["wa"], h["x"])
    for h in heads:
        h["dv"] = h["beta"] * h["w"]
        h["dm"] = jnp.where(row > col, -mm(h["w"], h["u"], NT), 0.0)
        h["dke"] = mm(h["u"], h["x"], NT)
    for h in heads:
        kn = h["kn"]
        km, ke = kn * h["minus"], kn * h["end"]
        dmb = h["beta"] * h["dm"]
        h["dbeta"] = jnp.sum(h["w"] * h["r"] + h["dm"] * h["kk"], axis=1, keepdims=True)
        dkp = mm(dmb, km) - mm(h["dv"], h["s"], NT)
        dkm = mm(dmb, h["kp"], TN) + h["dkm"]
        ended = h["dke"] * ke
        kept = jnp.sum((h["x"] * h["s"]).T, axis=0, keepdims=True) * jnp.exp(h["cum"][-1:])
        last = jnp.sum(ended, axis=0, keepdims=True) + kept
        dcum = h["dcum"] + dkp * h["kp"] - dkm * km - ended
        h["dg"] = sum_by(ones, dcum) + last
        grad = dkp * h["plus"] + dkm * h["minus"] + h["dke"] * h["end"]
        h["dk"] = unit_back(grad, kn, h["k_scale"])
    for h in heads:
        gate = sigmoid(h["gate_in"])
        h["dgate"] = h["dg"] * -h["rate"] * gate
        h["rate_row"] = -jnp.sum(h["dg"] * softplus(h["gate_in"]), axis=0, keepdims=True)
        h["bias_row"] = jnp.sum(h["dgate"], axis=0, keepdims=True)
    return heads


def column(table, index):
    lanes = lax.broadcasted_iota(jnp.int32, table.shape, 1)
    return jnp.sum(jnp.where(lanes == index, table, 0.0), axis=1, keepdims=True)


def local_kernel(
    group, hidden, down, up, beta_t, bias, rate, q, k, v, go, s,
    low, gates, dq, cum, wa, wb, u, r, kk, dcum, dkm, maps, adds,
):
    size = s.shape[-1]
    step = pl.program_id(0)

    @pl.when(step == 0)
    def _():
        low[...] = dot(hidden[...], down[...]).astype(BF16)
        gates[...] = sigmoid(dot(hidden[...], beta_t[...], NT))

    heads = []
    for i in range(group):
        at = slice(i * size, (i + 1) * size)
        heads.append(
            dict(
                q=q[:, at], k=k[:, at], v=v[:, at], go=go[:, at], s=s[i],
                gate_in=dot(low[...], up[i]) + bias[:, at],
                rate=rate[:, at],
                beta=column(gates[...], step * group + i),
            )
        )
    for i, h in enumerate(local_heads(heads)):
        at = slice(i * size, (i + 1) * size)
        dq[:, at] = h["dq"].astype(BF16)
        cum[i], wa[i], wb[i], u[i], r[i] = h["cum"], h["wa"].astype(BF16), h["wb"], h["u"].astype(BF16), h["r"]
        kk[i], dcum[i], dkm[i] = h["kk"], h["dcum"], h["dkm"]
        maps[i], adds[i] = h["map"], h["add"]


def back_kernel(
    group, shards, steps,
    hidden, down, up, beta_t, bias, rate, k, s, low, gates, x, cum, wa, wb, u, r, kk, dcum, dkm,
    dk, dv, dhidden, packed,
    low_sum, beta_cot, rows,
):
    size = s.shape[-1]
    count = group * steps
    step = pl.program_id(0)
    per_shard = count // shards
    deep = down.shape[0] // shards
    first_rep = deep + per_shard * size
    lanes = lax.broadcasted_iota(jnp.int32, beta_cot.shape, 1)

    @pl.when(step == 0)
    def _():
        low_sum[...] = jnp.zeros_like(low_sum)
        beta_cot[...] = jnp.zeros_like(beta_cot)

    heads = []
    for i in range(group):
        at = slice(i * size, (i + 1) * size)
        heads.append(
            dict(
                k=k[:, at], s=s[i], x=x[i].astype(F32),
                gate_in=dot(low[...], up[i]) + bias[:, at],
                rate=rate[:, at],
                beta=column(gates[...], step * group + i),
                cum=cum[i], wa=wa[i], wb=wb[i], u=u[i], r=r[i], kk=kk[i], dcum=dcum[i], dkm=dkm[i],
            )
        )
    for i, h in enumerate(back_heads(heads)):
        at = slice(i * size, (i + 1) * size)
        head = step * group + i
        dk[:, at] = h["dk"].astype(BF16)
        dv[:, at] = h["dv"].astype(BF16)
        half = h["dgate"].astype(BF16)
        place = pl.multiple_of(deep + (head % per_shard) * size, 16)
        packed[head // per_shard, pl.ds(place, size), :] = dot(low[...], half, TN).astype(BF16)
        low_sum[...] += dot(half, up[i], NT)
        beta_cot[...] += jnp.where(lanes == head, h["dbeta"], 0.0)
        rows[pl.ds(head, 1), :] = h["bias_row"]
        rows[pl.ds(count + head, 1), :] = h["rate_row"]

    @pl.when(step == steps - 1)
    def _():
        low_grad = low_sum[...].astype(BF16)
        gate = gates[...]
        score = (beta_cot[...] * gate * (1.0 - gate)).astype(BF16)
        dhidden[...] = (dot(low_grad, down[...], NT) + dot(score, beta_t[...])).astype(BF16)
        down_term = dot(hidden[...], low_grad, TN).astype(BF16)
        beta_term = dot(score, hidden[...], TN).astype(BF16)
        tail = rows[...].astype(BF16)
        blocks = hidden.shape[1] // size
        for shard in range(shards):
            packed[shard, :deep, :] = down_term[shard * deep : (shard + 1) * deep]
            for b in range(blocks):
                place = first_rep + b * count
                packed[shard, place : place + count, :] = beta_term[:, b * size : (b + 1) * size]
            place = first_rep + blocks * count
            packed[shard, place : place + 2 * count, :] = tail
            if place + 2 * count < packed.shape[1]:
                rest = packed.shape[1] - place - 2 * count
                packed[shard, place + 2 * count :, :] = jnp.zeros((rest, packed.shape[2]), BF16)


def chain_kernel(count, maps, adds, out, sent, got, send_sem, recv_sem):
    me = lax.axis_index("ctx")
    barrier = pltpu.get_barrier_semaphore()

    @pl.when(me > 0)
    def _():
        pl.semaphore_signal(barrier, inc=1, device_id={"ctx": me - 1}, device_id_type=MESH)

    @pl.when(me < count - 1)
    def _():
        pl.semaphore_signal(barrier, inc=1, device_id={"ctx": me + 1}, device_id_type=MESH)

    @pl.when((me > 0) & (me < count - 1))
    def _():
        pl.semaphore_wait(barrier, 2)

    @pl.when((me == 0) | (me == count - 1))
    def _():
        pl.semaphore_wait(barrier, 1)

    @pl.when(me == count - 1)
    def _():
        got[...] = jnp.zeros_like(got)

    def copy(head):
        return pltpu.make_async_remote_copy(
            src_ref=sent.at[head], dst_ref=got.at[head],
            send_sem=send_sem.at[head], recv_sem=recv_sem.at[head],
            device_id={"ctx": jnp.maximum(me - 1, 0)}, device_id_type=MESH,
        )

    def turn(head, _):
        @pl.when(me < count - 1)
        def _():
            copy(head).wait_recv()

        value = got[head]
        out[head] = value

        @pl.when(me > 0)
        def _():
            sent[head] = (adds[head] + mm(maps[head], value, NN, 3)).astype(BF16)
            copy(head).start()

        return 0

    lax.fori_loop(0, maps.shape[0], turn, 0)

    @pl.when(me > 0)
    def _():
        def done(head, _):
            copy(head).wait_send()
            return 0

        lax.fori_loop(0, maps.shape[0], done, 0)


def gather_kernel(shards, down, up, beta, down_all, up_all, beta_all, send_sem, recv_sem):
    me = lax.axis_index("fsdp")
    chips = shards // 2
    chip, core = me // 2, me % 2
    sibling = chip * 2 + (1 - core)
    peers = [lax.rem(chip + d, chips) * 2 + core for d in range(1, chips)]
    sources = [lax.rem(chip + chips - d, chips) * 2 + core for d in range(1, chips)]
    barrier = pltpu.get_barrier_semaphore()
    for other in [sibling] + peers:
        pl.semaphore_signal(barrier, inc=1, device_id={"fsdp": other}, device_id_type=MESH)
    size = up_all.shape[-1]
    for i in range(up.shape[1] // size):
        up_all[me, i] = up[:, i * size : (i + 1) * size]
    down_all[me] = down[...]
    beta_all[me] = beta[...]
    pl.semaphore_wait(barrier, chips)

    def copies(shard, target, slot):
        return [
            pltpu.make_async_remote_copy(
                src_ref=ref.at[shard], dst_ref=ref.at[shard],
                send_sem=send_sem.at[slot, i], recv_sem=recv_sem.at[slot, i],
                device_id={"fsdp": target}, device_id_type=MESH,
            )
            for i, ref in enumerate((down_all, up_all, beta_all))
        ]

    for d, peer in enumerate(peers):
        for c in copies(me, peer, 1 + d):
            c.start()
    for c in copies(me, sibling, 0):
        c.start()
    for d, source in enumerate(sources):
        for c, onward in zip(copies(source, peers[d], 1 + d), copies(source, sibling, chips + d)):
            c.wait_recv()
            onward.start()
    for c in copies(sibling, sibling, 0):
        c.wait_recv()
    for d, source in enumerate(sources):
        theirs = (source // 2) * 2 + (1 - core)
        for c in copies(theirs, sibling, chips + d):
            c.wait_recv()
    for slot in range(2 * chips - 1):
        for c in copies(me, sibling, slot):
            c.wait_send()


def reduce_kernel(
    shards, count, packed, out,
    core_got, core_sum, chip_got, chip_sum, piece_got, total, spread,
    core_send, core_recv, chip_send, chip_recv, piece_send, piece_recv, spread_send, spread_recv,
):
    me, mine = lax.axis_index("fsdp"), lax.axis_index("ctx")
    chips = shards // 2
    chip, core = me // 2, me % 2
    sibling = chip * 2 + (1 - core)
    peers = [lax.rem(chip + d, chips) * 2 + core for d in range(1, chips)]
    others = [lax.rem(mine + d, count) for d in range(1, count)]
    piece = packed.shape[1] // count
    barrier = pltpu.get_barrier_semaphore()
    for other in [sibling] + peers:
        pl.semaphore_signal(barrier, inc=1, device_id={"fsdp": other}, device_id_type=MESH)

    def greet(d, _):
        pl.semaphore_signal(
            barrier, inc=1, device_id={"ctx": lax.rem(mine + d, count)}, device_id_type=MESH
        )
        return 0

    lax.fori_loop(1, count, greet, 0)
    pl.semaphore_wait(barrier, chips + count - 1)

    def core_copy(c):
        return pltpu.make_async_remote_copy(
            src_ref=packed.at[c * 2 + (1 - core)], dst_ref=core_got.at[c],
            send_sem=core_send.at[c], recv_sem=core_recv.at[c],
            device_id={"fsdp": sibling}, device_id_type=MESH,
        )

    def chip_copy(d, peer):
        return pltpu.make_async_remote_copy(
            src_ref=core_sum.at[peer // 2], dst_ref=chip_got.at[d],
            send_sem=chip_send.at[d], recv_sem=chip_recv.at[d],
            device_id={"fsdp": peer}, device_id_type=MESH,
        )

    order = [peer // 2 for peer in peers] + [chip]
    for c in order:
        core_copy(c).start()
    for d, c in enumerate(order):
        core_copy(c).wait_recv()
        both = packed[c * 2 + core].astype(F32) + core_got[c].astype(F32)
        if d < chips - 1:
            core_sum[c] = both.astype(BF16)
            chip_copy(d, peers[d]).start()
        else:
            own = both
    for d in range(chips - 1):
        chip_copy(d, peers[d]).wait_recv()
        own = own + chip_got[d].astype(F32)
    chip_sum[...] = own.astype(BF16)

    def piece_copy(d):
        other = lax.rem(mine + d, count)
        at = pl.multiple_of(other * piece, 16)
        return pltpu.make_async_remote_copy(
            src_ref=chip_sum.at[pl.ds(at, piece)], dst_ref=piece_got.at[d - 1],
            send_sem=piece_send.at[d - 1], recv_sem=piece_recv.at[d - 1],
            device_id={"ctx": other}, device_id_type=MESH,
        )

    def spread_copy(d):
        return pltpu.make_async_remote_copy(
            src_ref=total, dst_ref=spread.at[d - 1],
            send_sem=spread_send.at[d - 1], recv_sem=spread_recv.at[d - 1],
            device_id={"ctx": lax.rem(mine + d, count)}, device_id_type=MESH,
        )

    def start_piece(d, _):
        piece_copy(d).start()
        return 0

    def add_piece(d, so_far):
        piece_copy(d).wait_recv()
        return so_far + piece_got[d - 1].astype(F32)

    def start_spread(d, _):
        spread_copy(d).start()
        return 0

    def place_spread(d, _):
        spread_copy(d).wait_recv()
        source = lax.rem(mine + count - d, count)
        out[pl.ds(pl.multiple_of(source * piece, 16), piece), :] = spread[d - 1].astype(F32)
        return 0

    def finish(d, _):
        piece_copy(d).wait_send()
        spread_copy(d).wait_send()
        return 0

    lax.fori_loop(1, count, start_piece, 0)
    at = pl.multiple_of(mine * piece, 16)
    summed = lax.fori_loop(1, count, add_piece, chip_sum[pl.ds(at, piece), :].astype(F32))
    total[...] = summed.astype(BF16)
    lax.fori_loop(1, count, start_spread, 0)
    out[pl.ds(at, piece), :] = total[...].astype(F32)
    lax.fori_loop(1, count, place_spread, 0)
    lax.fori_loop(1, count, finish, 0)
    for c in range(chips):
        core_copy(c).wait_send()
    for d, peer in enumerate(peers):
        chip_copy(d, peer).wait_send()


def vmem(count):
    return [pl.BlockSpec(memory_space=pltpu.VMEM)] * count


def remote(collective):
    return pltpu.CompilerParams(
        collective_id=collective, has_side_effects=True, vmem_limit_bytes=VMEM_LIMIT
    )


def on_device(
    shards, blocks_ctx,
    hidden, query_heads, key_heads, value_heads, out_grad, checkpoint,
    gate_down, gate_up, gate_bias, decay_rate, beta_weight,
):
    tokens, width = hidden.shape[1], hidden.shape[2]
    count, size = checkpoint.shape[2], checkpoint.shape[3]
    rank = gate_down.shape[1]
    deep = gate_down.shape[0]
    per_shard = count // shards
    chips = shards // 2
    hidden, q, k, v, go = (a[0] for a in (hidden, query_heads, key_heads, value_heads, out_grad))
    state = checkpoint[0, 0]
    bias, rate = gate_bias.reshape(1, -1), decay_rate.reshape(1, -1)
    dma = pltpu.SemaphoreType.DMA

    down_all, up_all, beta_all = pl.pallas_call(
        functools.partial(gather_kernel, shards),
        out_shape=(
            jax.ShapeDtypeStruct((shards, deep, rank), BF16),
            jax.ShapeDtypeStruct((shards, per_shard, rank, size), BF16),
            jax.ShapeDtypeStruct((shards, count, deep), BF16),
        ),
        in_specs=vmem(3),
        out_specs=tuple(vmem(3)),
        scratch_shapes=[dma((2 * chips - 1, 3)), dma((2 * chips - 1, 3))],
        compiler_params=remote(0),
        name="gather_weights",
    )(gate_down, gate_up, beta_weight.T)
    down_full = down_all.reshape(width, rank)
    up_full = up_all.reshape(count, rank, size)
    beta_t = beta_all.swapaxes(0, 1).reshape(count, width)

    group = 4 if count % 4 == 0 else 1
    steps = count // group
    whole = lambda *shape: pl.BlockSpec(shape, lambda i: (0,) * len(shape))
    cols = pl.BlockSpec((tokens, group * size), lambda i: (0, i))
    line = pl.BlockSpec((1, group * size), lambda i: (0, i))
    per_head = lambda a, b: pl.BlockSpec((group, a, b), lambda i: (i, 0, 0))
    of_heads = lambda a, b, kind: jax.ShapeDtypeStruct((count, a, b), kind)
    weights = [
        whole(tokens, width), whole(width, rank), per_head(rank, size), whole(count, width), line, line
    ]
    square = per_head(tokens, size)
    grid_params = pltpu.CompilerParams(
        dimension_semantics=("arbitrary",), vmem_limit_bytes=VMEM_LIMIT
    )
    low, gates, dq, cum, wa, wb, u, r, kk, dcum, dkm, maps, adds = pl.pallas_call(
        functools.partial(local_kernel, group),
        grid=(steps,),
        out_shape=(
            jax.ShapeDtypeStruct((tokens, rank), BF16),
            jax.ShapeDtypeStruct((tokens, count), F32),
            jax.ShapeDtypeStruct((tokens, count * size), BF16),
            of_heads(tokens, size, F32), of_heads(tokens, size, BF16), of_heads(tokens, size, F32),
            of_heads(tokens, size, BF16), of_heads(tokens, size, F32), of_heads(tokens, tokens, F32),
            of_heads(tokens, size, F32), of_heads(tokens, size, F32),
            of_heads(size, size, F32), of_heads(size, size, F32),
        ),
        in_specs=weights + [cols] * 4 + [per_head(size, size)],
        out_specs=(
            whole(tokens, rank), whole(tokens, count), cols,
            square, square, square, square, square, per_head(tokens, tokens), square, square,
            per_head(size, size), per_head(size, size),
        ),
        compiler_params=grid_params,
        name="local_terms",
    )(hidden, down_full, up_full, beta_t, bias, rate, q, k, v, go, state)

    end_grad = pl.pallas_call(
        functools.partial(chain_kernel, blocks_ctx),
        out_shape=of_heads(size, size, BF16),
        in_specs=vmem(2),
        out_specs=pl.BlockSpec(memory_space=pltpu.VMEM),
        scratch_shapes=[
            pltpu.VMEM((count, size, size), BF16), pltpu.VMEM((count, size, size), BF16),
            dma((count,)), dma((count,)),
        ],
        compiler_params=remote(1),
        name="state_chain",
    )(maps, adds)

    rows = deep + per_shard * size + (width // size) * count + 2 * count
    unit_rows = 16 * blocks_ctx
    rows = -(-rows // unit_rows) * unit_rows
    dk, dv, dhidden, packed = pl.pallas_call(
        functools.partial(back_kernel, group, shards, steps),
        grid=(steps,),
        out_shape=(
            jax.ShapeDtypeStruct((tokens, count * size), BF16),
            jax.ShapeDtypeStruct((tokens, count * size), BF16),
            jax.ShapeDtypeStruct((tokens, width), BF16),
            jax.ShapeDtypeStruct((shards, rows, size), BF16),
        ),
        in_specs=weights
        + [cols, per_head(size, size), whole(tokens, rank), whole(tokens, count), per_head(size, size)]
        + [square] * 5
        + [per_head(tokens, tokens), square, square],
        out_specs=(cols, cols, whole(tokens, width), whole(shards, rows, size)),
        scratch_shapes=[
            pltpu.VMEM((tokens, rank), F32), pltpu.VMEM((tokens, count), F32),
            pltpu.VMEM((2 * count, size), F32),
        ],
        compiler_params=grid_params,
        name="block_pullback",
    )(hidden, down_full, up_full, beta_t, bias, rate, k, state, low, gates, end_grad,
      cum, wa, wb, u, r, kk, dcum, dkm)

    piece = rows // blocks_ctx
    summed = pl.pallas_call(
        functools.partial(reduce_kernel, shards, blocks_ctx),
        out_shape=jax.ShapeDtypeStruct((rows, size), F32),
        in_specs=vmem(1),
        out_specs=pl.BlockSpec(memory_space=pltpu.VMEM),
        scratch_shapes=[
            pltpu.VMEM((chips, rows, size), BF16), pltpu.VMEM((chips, rows, size), BF16),
            pltpu.VMEM((max(chips - 1, 1), rows, size), BF16), pltpu.VMEM((rows, size), BF16),
            pltpu.VMEM((blocks_ctx - 1, piece, size), BF16), pltpu.VMEM((piece, size), BF16),
            pltpu.VMEM((blocks_ctx - 1, piece, size), BF16),
            dma((chips,)), dma((chips,)), dma((max(chips - 1, 1),)), dma((max(chips - 1, 1),)),
            dma((blocks_ctx - 1,)), dma((blocks_ctx - 1,)),
            dma((blocks_ctx - 1,)), dma((blocks_ctx - 1,)),
        ],
        compiler_params=remote(2),
        name="reduce_weights",
    )(packed)

    up_at = deep + per_shard * size
    beta_at = up_at + (width // size) * count
    up_grad = summed[deep:up_at].reshape(per_shard, rank, size).swapaxes(0, 1).reshape(rank, -1)
    beta_rows = summed[up_at:beta_at].reshape(width // size, count, size)
    beta_full = beta_rows.swapaxes(1, 2).reshape(width, count)
    beta_grad = lax.dynamic_slice_in_dim(beta_full, lax.axis_index("fsdp") * deep, deep, 0)
    vectors = summed[beta_at : beta_at + 2 * count].reshape(2, count * size)
    return (
        dq[None], dk[None], dv[None], dhidden[None],
        summed[:deep], up_grad, beta_grad, vectors[0], vectors[1],
    )


def solution(mesh):
    shards, blocks_ctx = mesh.shape["fsdp"], mesh.shape["ctx"]
    tokens, state = P("fsdp", "ctx", None), P("fsdp", "ctx", None, None, None)
    by_row, by_col = P("fsdp", None), P(None, "fsdp")
    return jax.shard_map(
        functools.partial(on_device, shards, blocks_ctx),
        mesh=mesh,
        in_specs=(tokens,) * 5 + (state, by_row, by_col, P(), P(), by_row),
        out_specs=(tokens,) * 4 + (by_row, by_col, by_row, P(), P()),
        check_vma=False,
    )
```

```python
import functools

import jax
import jax.numpy as jnp
from jax import lax
from jax.experimental import pallas as pl
from jax.experimental.pallas import tpu as pltpu
from jax.sharding import PartitionSpec as P

EPSILON = 1e-06
MESH = pl.DeviceIdType.MESH
F32, BF16 = jnp.float32, jnp.bfloat16
VMEM_LIMIT = 48 * 1024 * 1024
NN, NT, TN = ((1,), (0,)), ((1,), (1,)), ((0,), (0,))
INV_PASSES = 1
PASSES = 3


def dot(left, right, dims=NN):
    return lax.dot_general(left, right, (dims, ((), ())), preferred_element_type=F32)


def halves(value):
    if value.dtype == BF16:
        return value, None
    high = value.astype(BF16)
    return high, (value - high.astype(F32)).astype(BF16)


def mm(left, right, dims=NN, passes=None):
    passes = PASSES if passes is None else passes
    if passes == 1:
        return dot(left.astype(BF16), right.astype(BF16), dims)
    left_high, left_low = halves(left)
    right_high, right_low = halves(right)
    total = dot(left_high, right_high, dims)
    if left_low is not None:
        total += dot(left_low, right_high, dims)
    if right_low is not None:
        total += dot(left_high, right_low, dims)
    return total


def sum_by(ones, value):
    high = value.astype(BF16)
    rest = value - high.astype(F32)
    mid = rest.astype(BF16)
    low = (rest - mid.astype(F32)).astype(BF16)
    return dot(ones, high) + dot(ones, mid) + dot(ones, low)


def iotas(size):
    return (
        lax.broadcasted_iota(jnp.int32, (size, size), 0),
        lax.broadcasted_iota(jnp.int32, (size, size), 1),
    )


def inverse(systems):
    size = systems[0].shape[0]
    row, col = iotas(size)
    eye = jnp.where(row == col, 1.0, 0.0)

    def off(block):
        same = row // (2 * block) == col // (2 * block)
        return same & ((row // block) % 2 == 1) & ((col // block) % 2 == 0)

    found = [eye - jnp.where(off(1), system, 0.0) for system in systems]
    block = 2
    while block < size:
        mask = off(block)
        parts = [mm(jnp.where(mask, s, 0.0), t, NN, INV_PASSES) for s, t in zip(systems, found)]
        found = [t - mm(t, p, NN, INV_PASSES) for t, p in zip(found, parts)]
        block *= 2
    return found


def softplus(value):
    return jnp.maximum(value, 0.0) + jnp.log1p(jnp.exp(-jnp.abs(value)))


def sigmoid(value):
    return 1.0 / (1.0 + jnp.exp(-value))


def unit(rows):
    scale = lax.rsqrt(jnp.sum(rows * rows, axis=-1, keepdims=True) + EPSILON)
    return rows * scale, scale


def unit_back(grad, rows, scale):
    return scale * (grad - rows * jnp.sum(grad * rows, axis=-1, keepdims=True))


def head_terms(keys, gate_in, rate):
    size = keys.shape[0]
    row, col = iotas(size)
    kn, k_scale = unit(keys.astype(F32))
    ones = jnp.where(row >= col, 1.0, 0.0).astype(BF16)
    cumulative = sum_by(ones, -rate * softplus(gate_in))
    return kn, k_scale, cumulative


def first_heads(heads):
    row, col = iotas(heads[0]["k"].shape[0])
    for h in heads:
        kn, _, cum = head_terms(h["k"], h["gate_in"], h["rate"])
        qn, _ = unit(h["q"].astype(F32))
        plus = jnp.exp(cum)
        h.update(cum=cum, kp=kn * plus, km=kn * jnp.exp(-cum), qp=qn * plus)
        h.update(ke=kn * jnp.exp(cum[-1:] - cum))
    for h in heads:
        h["kk"] = jnp.where(row > col, mm(h["kp"], h["km"], NT), 0.0)
        h["p"] = jnp.where(row >= col, mm(h["qp"], h["km"], NT), 0.0)
    for h, t in zip(heads, inverse([h["kk"] * h["beta"] for h in heads])):
        h["t"] = t
    for h in heads:
        h["pg"] = mm(h["p"], h["go"], TN)
    for h in heads:
        h["wa"] = mm(h["t"], h["ke"], TN)
        h["wb"] = mm(h["t"], h["pg"], TN)
    for h in heads:
        kb = h["kp"] * h["beta"]
        end = jnp.exp(h["cum"][-1:])
        h["map"] = jnp.where(row == col, end, 0.0) - mm(kb, h["wa"], TN)
        h["add"] = mm(h["qp"], h["go"], TN) - mm(kb, h["wb"], TN)
    return heads


def rest_heads(heads):
    row, col = iotas(heads[0]["k"].shape[0])
    for h in heads:
        kn, _ = unit(h["k"].astype(F32))
        qn, q_scale = unit(h["q"].astype(F32))
        plus = jnp.exp(h["cum"])
        h.update(plus=plus, qn=qn, q_scale=q_scale)
        h.update(kp=kn * plus, km=kn * jnp.exp(-h["cum"]), qp=qn * plus)
        h["r"] = h["v"].astype(F32) - mm(h["kp"], h["s"])
    for h in heads:
        h["u"] = mm(h["t"], h["beta"] * h["r"])
    for h in heads:
        h["dp"] = jnp.where(row >= col, mm(h["go"], h["u"], NT), 0.0)
    for h in heads:
        dqp = mm(h["go"], h["s"], NT) + mm(h["dp"], h["km"])
        h["dq"] = unit_back(dqp * h["plus"], h["qn"], h["q_scale"])
        h["dcum"] = dqp * h["qp"]
        h["dkm"] = mm(h["dp"], h["qp"], TN)
    return heads


def back_heads(heads):
    size = heads[0]["k"].shape[0]
    row, col = iotas(size)
    ones = jnp.where(row <= col, 1.0, 0.0).astype(BF16)
    for h in heads:
        kn, k_scale = unit(h["k"].astype(F32))
        cum = h["cum"]
        plus, minus, end = jnp.exp(cum), jnp.exp(-cum), jnp.exp(cum[-1:] - cum)
        h.update(kn=kn, k_scale=k_scale, plus=plus, minus=minus, end=end, kp=kn * plus)
        h["w"] = h["wb"] + mm(h["wa"], h["x"])
    for h in heads:
        h["dv"] = h["beta"] * h["w"]
        h["dm"] = jnp.where(row > col, -mm(h["w"], h["u"], NT), 0.0)
        h["dke"] = mm(h["u"], h["x"], NT)
    for h in heads:
        kn = h["kn"]
        km, ke = kn * h["minus"], kn * h["end"]
        dmb = h["beta"] * h["dm"]
        h["dbeta"] = jnp.sum(h["w"] * h["r"] + h["dm"] * h["kk"], axis=1, keepdims=True)
        dkp = mm(dmb, km) - mm(h["dv"], h["s"], NT)
        dkm = mm(dmb, h["kp"], TN) + h["dkm"]
        ended = h["dke"] * ke
        kept = jnp.sum((h["x"] * h["s"]).T, axis=0, keepdims=True) * jnp.exp(h["cum"][-1:])
        last = jnp.sum(ended, axis=0, keepdims=True) + kept
        dcum = h["dcum"] + dkp * h["kp"] - dkm * km - ended
        h["dg"] = sum_by(ones, dcum) + last
        grad = dkp * h["plus"] + dkm * h["minus"] + h["dke"] * h["end"]
        h["dk"] = unit_back(grad, kn, h["k_scale"])
    for h in heads:
        gate = sigmoid(h["gate_in"])
        h["dgate"] = h["dg"] * -h["rate"] * gate
        h["rate_row"] = -jnp.sum(h["dg"] * softplus(h["gate_in"]), axis=0, keepdims=True)
        h["bias_row"] = jnp.sum(h["dgate"], axis=0, keepdims=True)
    return heads


def column(table, index):
    lanes = lax.broadcasted_iota(jnp.int32, table.shape, 1)
    return jnp.sum(jnp.where(lanes == index, table, 0.0), axis=1, keepdims=True)


def fused_kernel(
    shards, count_ctx, group,
    hidden_in, q_in, k_in, v_in, go_in, s_in, down_in, up_in, beta_in, bias, rate,
    dq_out, dk_out, dv_out, dhidden_out, out,
    hidden, q, k, v, go, s, dq, dk, dv, dhidden, down_all, up_all, beta_all, beta_full,
    low, gates, cum, t, wa, wb, u, r, kk, dcum, dkm, maps, adds, sent, got,
    low_sum, beta_cot, rows, packed,
    core_got, core_sum, chip_got, chip_sum, piece_got, total, spread,
    load_sem, store_sem, gather_send, gather_recv, chain_send, chain_recv,
    core_send, core_recv, chip_send, chip_recv, piece_send, piece_recv, spread_send, spread_recv,
):
    me, mine = lax.axis_index("fsdp"), lax.axis_index("ctx")
    chips = shards // 2
    chip, core = me // 2, me % 2
    sibling = chip * 2 + (1 - core)
    peers = [lax.rem(chip + d, chips) * 2 + core for d in range(1, chips)]
    sources = [lax.rem(chip + chips - d, chips) * 2 + core for d in range(1, chips)]
    piece = packed.shape[1] // count_ctx
    count, size = s.shape[0], s.shape[-1]
    groups = count // group
    per_shard = count // shards
    deep = down_all.shape[1]
    first_rep = deep + per_shard * size

    loads = [
        pltpu.make_async_copy(src, dst, load_sem.at[i])
        for i, (src, dst) in enumerate(
            ((hidden_in, hidden), (k_in, k), (q_in, q), (go_in, go), (s_in, s), (v_in, v))
        )
    ]
    for c in loads:
        c.start()
    barrier = pltpu.get_barrier_semaphore()
    for other in [sibling] + peers:
        pl.semaphore_signal(barrier, inc=1, device_id={"fsdp": other}, device_id_type=MESH)

    def greet(d, _):
        pl.semaphore_signal(
            barrier, inc=1, device_id={"ctx": lax.rem(mine + d, count_ctx)}, device_id_type=MESH
        )
        return 0

    lax.fori_loop(1, count_ctx, greet, 0)
    for i in range(per_shard):
        up_all[me, i] = up_in[:, i * size : (i + 1) * size]
    down_all[me] = down_in[...]
    beta_all[me] = beta_in[...]
    low_sum[...] = jnp.zeros_like(low_sum)
    beta_cot[...] = jnp.zeros_like(beta_cot)

    @pl.when(mine == count_ctx - 1)
    def _():
        got[...] = jnp.zeros_like(got)

    pl.semaphore_wait(barrier, chips + count_ctx - 1)

    def copies(shard, target, slot):
        return [
            pltpu.make_async_remote_copy(
                src_ref=ref.at[shard], dst_ref=ref.at[shard],
                send_sem=gather_send.at[slot, i], recv_sem=gather_recv.at[slot, i],
                device_id={"fsdp": target}, device_id_type=MESH,
            )
            for i, ref in enumerate((down_all, beta_all, up_all))
        ]

    for d, peer in enumerate(peers):
        for c in copies(me, peer, 1 + d):
            c.start()
    for c in copies(me, sibling, 0):
        c.start()
    for d, source in enumerate(sources):
        for c, onward in zip(copies(source, peers[d], 1 + d), copies(source, sibling, chips + d)):
            c.wait_recv()
            onward.start()
    for c in copies(sibling, sibling, 0):
        c.wait_recv()
    for d, source in enumerate(sources):
        theirs = (source // 2) * 2 + (1 - core)
        for c in copies(theirs, sibling, chips + d):
            c.wait_recv()
    for c in loads:
        c.wait()

    for shard in range(shards):
        turned = beta_all[shard].astype(F32).T
        beta_full[shard * deep : (shard + 1) * deep, :] = turned[:deep].astype(BF16)
    low[...] = dot(hidden[...], down_all[...].reshape(shards * deep, -1)).astype(BF16)
    gates[...] = sigmoid(dot(hidden[...], beta_full[...]))

    def chain_copy(head):
        return pltpu.make_async_remote_copy(
            src_ref=sent.at[head], dst_ref=got.at[head],
            send_sem=chain_send.at[head], recv_sem=chain_recv.at[head],
            device_id={"ctx": jnp.maximum(mine - 1, 0)}, device_id_type=MESH,
        )

    hop = count_ctx - 1 - mine
    late = jnp.minimum(groups + 1 + 2 * (hop - groups), 2 * groups - 1)
    first_slot = jnp.where(hop < groups, hop, late)

    def chain_turn(head, _):
        @pl.when(mine < count_ctx - 1)
        def _():
            chain_copy(head).wait_recv()

        @pl.when(mine > 0)
        def _():
            sent[head] = (adds[head] + mm(maps[head], got[head], NN, 3)).astype(BF16)
            chain_copy(head).start()

        return 0

    def chain(slot):
        part = slot - first_slot

        @pl.when((part >= 0) & (part < groups))
        def _():
            lax.fori_loop(part * group, part * group + group, chain_turn, 0)

    def take(g, i):
        head = g * group + i
        at = pl.ds(pl.multiple_of(head * size, size), size)
        return head, at, dict(rate=rate[:, at], beta=column(gates[...], head))

    def gate_in(head, at):
        return dot(low[...], up_all[head // per_shard, head % per_shard]) + bias[:, at]

    def first(g, _):
        heads = []
        for i in range(group):
            head, at, h = take(g, i)
            h.update(q=q[:, at], k=k[:, at], go=go[:, at], gate_in=gate_in(head, at))
            heads.append(h)
        for i, h in enumerate(first_heads(heads)):
            n = g * group + i
            cum[n], kk[n], t[n], wa[n], wb[n] = h["cum"], h["kk"], h["t"], h["wa"].astype(BF16), h["wb"]
            maps[n], adds[n] = h["map"], h["add"]
        chain(g)
        return 0

    def rest(g, _):
        heads = []
        for i in range(group):
            head, at, h = take(g, i)
            h.update(q=q[:, at], k=k[:, at], v=v[:, at], go=go[:, at])
            h.update(s=s[head], cum=cum[head], t=t[head])
            heads.append(h)
        for i, h in enumerate(rest_heads(heads)):
            n, at, _ = take(g, i)
            dq[:, at] = h["dq"].astype(BF16)
            u[n], r[n], dcum[n], dkm[n] = h["u"].astype(BF16), h["r"], h["dcum"], h["dkm"]
        chain(groups + g)
        return 0

    lanes = lax.broadcasted_iota(jnp.int32, beta_cot.shape, 1)

    def back(g, _):
        heads = []
        for i in range(group):
            n, at, h = take(g, i)
            h.update(k=k[:, at], s=s[n], x=got[n].astype(F32), gate_in=gate_in(n, at))
            h.update(cum=cum[n], wa=wa[n], wb=wb[n], u=u[n], r=r[n], kk=kk[n], dcum=dcum[n], dkm=dkm[n])
            heads.append(h)
        for i, h in enumerate(back_heads(heads)):
            head, at, _ = take(g, i)
            dk[:, at] = h["dk"].astype(BF16)
            dv[:, at] = h["dv"].astype(BF16)
            half = h["dgate"].astype(BF16)
            place = pl.multiple_of(deep + (head % per_shard) * size, 16)
            packed[head // per_shard, pl.ds(place, size), :] = dot(low[...], half, TN).astype(BF16)
            low_sum[...] += dot(half, up_all[head // per_shard, head % per_shard], NT)
            beta_cot[...] += jnp.where(lanes == head, h["dbeta"], 0.0)
            rows[pl.ds(head, 1), :] = h["bias_row"]
            rows[pl.ds(count + head, 1), :] = h["rate_row"]
        chain(2 * groups + g)
        return 0

    stores = [
        pltpu.make_async_copy(src, dst, store_sem.at[i])
        for i, (src, dst) in enumerate(
            ((dq, dq_out), (dk, dk_out), (dv, dv_out), (dhidden, dhidden_out))
        )
    ]
    lax.fori_loop(0, groups, first, 0)
    lax.fori_loop(0, groups, rest, 0)
    stores[0].start()
    lax.fori_loop(0, groups, back, 0)
    stores[1].start()
    stores[2].start()

    low_grad = low_sum[...].astype(BF16)
    gate = gates[...]
    score = (beta_cot[...] * gate * (1.0 - gate)).astype(BF16)
    down_term = dot(hidden[...], low_grad, TN).astype(BF16)
    beta_term = dot(score, hidden[...], TN).astype(BF16)
    tail = rows[...].astype(BF16)
    blocks = hidden.shape[1] // size
    for shard in range(shards):
        packed[shard, :deep, :] = down_term[shard * deep : (shard + 1) * deep]
        for b in range(blocks):
            place = first_rep + b * count
            packed[shard, place : place + count, :] = beta_term[:, b * size : (b + 1) * size]
        place = first_rep + blocks * count
        packed[shard, place : place + 2 * count, :] = tail
        if place + 2 * count < packed.shape[1]:
            left = packed.shape[1] - place - 2 * count
            packed[shard, place + 2 * count :, :] = jnp.zeros((left, packed.shape[2]), BF16)

    def core_copy(c):
        return pltpu.make_async_remote_copy(
            src_ref=packed.at[c * 2 + (1 - core)], dst_ref=core_got.at[c],
            send_sem=core_send.at[c], recv_sem=core_recv.at[c],
            device_id={"fsdp": sibling}, device_id_type=MESH,
        )

    def chip_copy(d, peer):
        return pltpu.make_async_remote_copy(
            src_ref=core_sum.at[peer // 2], dst_ref=chip_got.at[d],
            send_sem=chip_send.at[d], recv_sem=chip_recv.at[d],
            device_id={"fsdp": peer}, device_id_type=MESH,
        )

    order = [peer // 2 for peer in peers] + [chip]
    for c in order:
        core_copy(c).start()
    dhidden[...] = (
        dot(low_grad, down_all[...].reshape(shards * deep, -1), NT) + dot(score, beta_full[...], NT)
    ).astype(BF16)
    stores[3].start()
    for d, c in enumerate(order):
        core_copy(c).wait_recv()
        both = packed[c * 2 + core].astype(F32) + core_got[c].astype(F32)
        if d < chips - 1:
            core_sum[c] = both.astype(BF16)
            chip_copy(d, peers[d]).start()
        else:
            own = both
    for d in range(chips - 1):
        chip_copy(d, peers[d]).wait_recv()
        own = own + chip_got[d].astype(F32)
    chip_sum[...] = own.astype(BF16)

    def piece_copy(d):
        other = lax.rem(mine + d, count_ctx)
        at = pl.multiple_of(other * piece, 16)
        return pltpu.make_async_remote_copy(
            src_ref=chip_sum.at[pl.ds(at, piece)], dst_ref=piece_got.at[d - 1],
            send_sem=piece_send.at[d - 1], recv_sem=piece_recv.at[d - 1],
            device_id={"ctx": other}, device_id_type=MESH,
        )

    def spread_copy(d):
        return pltpu.make_async_remote_copy(
            src_ref=total, dst_ref=spread.at[d - 1],
            send_sem=spread_send.at[d - 1], recv_sem=spread_recv.at[d - 1],
            device_id={"ctx": lax.rem(mine + d, count_ctx)}, device_id_type=MESH,
        )

    def start_piece(d, _):
        piece_copy(d).start()
        return 0

    def add_piece(d, so_far):
        piece_copy(d).wait_recv()
        return so_far + piece_got[d - 1].astype(F32)

    def start_spread(d, _):
        spread_copy(d).start()
        return 0

    def place_spread(d, _):
        spread_copy(d).wait_recv()
        source = lax.rem(mine + count_ctx - d, count_ctx)
        out[pl.ds(pl.multiple_of(source * piece, 16), piece), :] = spread[d - 1].astype(F32)
        return 0

    def finish(d, _):
        piece_copy(d).wait_send()
        spread_copy(d).wait_send()
        return 0

    lax.fori_loop(1, count_ctx, start_piece, 0)
    at = pl.multiple_of(mine * piece, 16)
    summed = lax.fori_loop(1, count_ctx, add_piece, chip_sum[pl.ds(at, piece), :].astype(F32))
    total[...] = summed.astype(BF16)
    lax.fori_loop(1, count_ctx, start_spread, 0)
    out[pl.ds(at, piece), :] = total[...].astype(F32)
    lax.fori_loop(1, count_ctx, place_spread, 0)
    lax.fori_loop(1, count_ctx, finish, 0)
    for c in range(chips):
        core_copy(c).wait_send()
    for d, peer in enumerate(peers):
        chip_copy(d, peer).wait_send()
    for slot in range(2 * chips - 1):
        for c in copies(me, sibling, slot):
            c.wait_send()

    @pl.when(mine > 0)
    def _():
        def done(head, _):
            chain_copy(head).wait_send()
            return 0

        lax.fori_loop(0, count, done, 0)

    for c in stores:
        c.wait()


def vmem(count):
    return [pl.BlockSpec(memory_space=pltpu.VMEM)] * count


def remote(collective):
    return pltpu.CompilerParams(
        collective_id=collective, has_side_effects=True, vmem_limit_bytes=VMEM_LIMIT
    )


def on_device(
    shards, blocks_ctx,
    hidden, query_heads, key_heads, value_heads, out_grad, checkpoint,
    gate_down, gate_up, gate_bias, decay_rate, beta_weight,
):
    tokens, width = hidden.shape[1], hidden.shape[2]
    count, size = checkpoint.shape[2], checkpoint.shape[3]
    rank = gate_down.shape[1]
    deep = gate_down.shape[0]
    per_shard = count // shards
    chips = shards // 2
    hidden, q, k, v, go = (a[0] for a in (hidden, query_heads, key_heads, value_heads, out_grad))
    state = checkpoint[0, 0]
    bias, rate = gate_bias.reshape(1, -1), decay_rate.reshape(1, -1)
    dma = pltpu.SemaphoreType.DMA

    group = 4 if count % 4 == 0 else 1
    rows = deep + per_shard * size + (width // size) * count + 2 * count
    unit_size = 16 * blocks_ctx
    rows = -(-rows // unit_size) * unit_size
    piece = rows // blocks_ctx
    far = max(chips - 1, 1)
    wide = -(-deep // size) * size
    beta_t = jnp.pad(beta_weight.T, ((0, 0), (0, wide - deep)))
    channels = count * size
    anywhere = pl.BlockSpec(memory_space=pl.ANY)
    heads_f32 = pltpu.VMEM((count, tokens, size), F32)
    heads_bf16 = pltpu.VMEM((count, tokens, size), BF16)
    states_f32 = pltpu.VMEM((count, size, size), F32)
    states_bf16 = pltpu.VMEM((count, size, size), BF16)
    mixed = pltpu.VMEM((count, tokens, tokens), F32)
    sided = pltpu.VMEM((tokens, channels), BF16)
    sized = pltpu.VMEM((tokens, width), BF16)
    dq, dk, dv, dhidden, summed = pl.pallas_call(
        functools.partial(fused_kernel, shards, blocks_ctx, group),
        out_shape=(
            jax.ShapeDtypeStruct((tokens, channels), BF16),
            jax.ShapeDtypeStruct((tokens, channels), BF16),
            jax.ShapeDtypeStruct((tokens, channels), BF16),
            jax.ShapeDtypeStruct((tokens, width), BF16),
            jax.ShapeDtypeStruct((rows, size), F32),
        ),
        in_specs=[anywhere] * 6 + vmem(5),
        out_specs=(anywhere,) * 4 + (pl.BlockSpec(memory_space=pltpu.VMEM),),
        scratch_shapes=[
            sized, sided, sided, sided, sided, states_f32, sided, sided, sided, sized,
            pltpu.VMEM((shards, deep, rank), BF16),
            pltpu.VMEM((shards, per_shard, rank, size), BF16),
            pltpu.VMEM((shards, count, wide), BF16), pltpu.VMEM((width, count), BF16),
            pltpu.VMEM((tokens, rank), BF16), pltpu.VMEM((tokens, count), F32),
            heads_f32, mixed, heads_bf16, heads_f32, heads_bf16, heads_f32, mixed, heads_f32, heads_f32,
            states_f32, states_f32, states_bf16, states_bf16,
            pltpu.VMEM((tokens, rank), F32), pltpu.VMEM((tokens, count), F32),
            pltpu.VMEM((2 * count, size), F32), pltpu.VMEM((shards, rows, size), BF16),
            pltpu.VMEM((chips, rows, size), BF16), pltpu.VMEM((chips, rows, size), BF16),
            pltpu.VMEM((far, rows, size), BF16), pltpu.VMEM((rows, size), BF16),
            pltpu.VMEM((blocks_ctx - 1, piece, size), BF16), pltpu.VMEM((piece, size), BF16),
            pltpu.VMEM((blocks_ctx - 1, piece, size), BF16),
            dma((6,)), dma((4,)), dma((2 * chips - 1, 3)), dma((2 * chips - 1, 3)),
            dma((count,)), dma((count,)),
            dma((chips,)), dma((chips,)), dma((far,)), dma((far,)),
            dma((blocks_ctx - 1,)), dma((blocks_ctx - 1,)),
            dma((blocks_ctx - 1,)), dma((blocks_ctx - 1,)),
        ],
        compiler_params=remote(0),
        name="delta_backward",
    )(hidden, q, k, v, go, state, gate_down, gate_up, beta_t, bias, rate)

    up_at = deep + per_shard * size
    beta_at = up_at + (width // size) * count
    up_grad = summed[deep:up_at].reshape(per_shard, rank, size).swapaxes(0, 1).reshape(rank, -1)
    beta_rows = summed[up_at:beta_at].reshape(width // size, count, size)
    beta_full = beta_rows.swapaxes(1, 2).reshape(width, count)
    beta_grad = lax.dynamic_slice_in_dim(beta_full, lax.axis_index("fsdp") * deep, deep, 0)
    vectors = summed[beta_at : beta_at + 2 * count].reshape(2, count * size)
    return (
        dq[None], dk[None], dv[None], dhidden[None],
        summed[:deep], up_grad, beta_grad, vectors[0], vectors[1],
    )


def solution(mesh):
    shards, blocks_ctx = mesh.shape["fsdp"], mesh.shape["ctx"]
    tokens, state = P("fsdp", "ctx", None), P("fsdp", "ctx", None, None, None)
    by_row, by_col = P("fsdp", None), P(None, "fsdp")
    return jax.shard_map(
        functools.partial(on_device, shards, blocks_ctx),
        mesh=mesh,
        in_specs=(tokens,) * 5 + (state, by_row, by_col, P(), P(), by_row),
        out_specs=(tokens,) * 4 + (by_row, by_col, by_row, P(), P()),
        check_vma=False,
    )
```

```python
import functools

import jax
import jax.numpy as jnp
from jax import lax
from jax.experimental import pallas as pl
from jax.experimental.pallas import tpu as pltpu
from jax.sharding import PartitionSpec as P

EPSILON = 1e-06
MESH = pl.DeviceIdType.MESH
F32, BF16 = jnp.float32, jnp.bfloat16
VMEM_LIMIT = 60 * 1024 * 1024
NN, NT, TN = ((1,), (0,)), ((1,), (1,)), ((0,), (0,))
INV_PASSES = 1
PASSES = 3


def dot(left, right, dims=NN):
    return lax.dot_general(left, right, (dims, ((), ())), preferred_element_type=F32)


def halves(value):
    if value.dtype == BF16:
        return value, None
    high = value.astype(BF16)
    return high, (value - high.astype(F32)).astype(BF16)


def mm(left, right, dims=NN, passes=None):
    passes = PASSES if passes is None else passes
    if passes == 1:
        return dot(left.astype(BF16), right.astype(BF16), dims)
    left_high, left_low = halves(left)
    right_high, right_low = halves(right)
    lefts, rights = [left_high], [right_high]
    if left_low is not None:
        lefts, rights = lefts + [left_low], rights + [right_high]
    if right_low is not None:
        lefts, rights = lefts + [left_high], rights + [right_low]
    return dot(
        jnp.concatenate(lefts, axis=dims[0][0]), jnp.concatenate(rights, axis=dims[1][0]), dims
    )


def sum_by(ones, value):
    high = value.astype(BF16)
    rest = value - high.astype(F32)
    mid = rest.astype(BF16)
    low = (rest - mid.astype(F32)).astype(BF16)
    return dot(jnp.concatenate([ones] * 3, axis=1), jnp.concatenate([high, mid, low], axis=0))


def iotas(size):
    return (
        lax.broadcasted_iota(jnp.int32, (size, size), 0),
        lax.broadcasted_iota(jnp.int32, (size, size), 1),
    )


def inverse(systems):
    size = systems[0].shape[0]
    row, col = iotas(size)
    eye = jnp.where(row == col, 1.0, 0.0)

    def off(block):
        same = row // (2 * block) == col // (2 * block)
        return same & ((row // block) % 2 == 1) & ((col // block) % 2 == 0)

    found = [eye - jnp.where(off(1), system, 0.0) for system in systems]
    block = 2
    while block < size:
        mask = off(block)
        parts = [mm(jnp.where(mask, s, 0.0), t, NN, INV_PASSES) for s, t in zip(systems, found)]
        found = [t - mm(t, p, NN, INV_PASSES) for t, p in zip(found, parts)]
        block *= 2
    return found


def softplus(value):
    return jnp.maximum(value, 0.0) + jnp.log1p(jnp.exp(-jnp.abs(value)))


def sigmoid(value):
    return 1.0 / (1.0 + jnp.exp(-value))


def unit(rows):
    scale = lax.rsqrt(jnp.sum(rows * rows, axis=-1, keepdims=True) + EPSILON)
    return rows * scale, scale


def unit_back(grad, rows, scale):
    return scale * (grad - rows * jnp.sum(grad * rows, axis=-1, keepdims=True))


def head_terms(keys, gate_in, rate):
    size = keys.shape[0]
    row, col = iotas(size)
    kn, k_scale = unit(keys.astype(F32))
    ones = jnp.where(row >= col, 1.0, 0.0).astype(BF16)
    cumulative = sum_by(ones, -rate * softplus(gate_in))
    return kn, k_scale, cumulative


def first_heads(heads):
    row, col = iotas(heads[0]["k"].shape[0])
    for h in heads:
        kn, _, cum = head_terms(h["k"], h["gate_in"], h["rate"])
        qn, _ = unit(h["q"].astype(F32))
        plus = jnp.exp(cum)
        h.update(cum=cum, kp=kn * plus, km=kn * jnp.exp(-cum), qp=qn * plus)
        h.update(ke=kn * jnp.exp(cum[-1:] - cum))
    for h in heads:
        h["kk"] = jnp.where(row > col, mm(h["kp"], h["km"], NT), 0.0)
        h["p"] = jnp.where(row >= col, mm(h["qp"], h["km"], NT), 0.0)
    for h, t in zip(heads, inverse([h["kk"] * h["beta"] for h in heads])):
        h["t"] = t
    for h in heads:
        h["pg"] = mm(h["p"], h["go"], TN)
    for h in heads:
        h["wa"] = mm(h["t"], h["ke"], TN)
        h["wb"] = mm(h["t"], h["pg"], TN)
    for h in heads:
        kb = h["kp"] * h["beta"]
        end = jnp.exp(h["cum"][-1:])
        h["map"] = jnp.where(row == col, end, 0.0) - mm(kb, h["wa"], TN)
        h["add"] = mm(h["qp"], h["go"], TN) - mm(kb, h["wb"], TN)
    return heads


def rest_heads(heads):
    row, col = iotas(heads[0]["k"].shape[0])
    for h in heads:
        kn, _ = unit(h["k"].astype(F32))
        qn, q_scale = unit(h["q"].astype(F32))
        plus = jnp.exp(h["cum"])
        h.update(plus=plus, qn=qn, q_scale=q_scale)
        h.update(kp=kn * plus, km=kn * jnp.exp(-h["cum"]), qp=qn * plus)
        h["r"] = h["v"].astype(F32) - mm(h["kp"], h["s"])
    for h in heads:
        h["u"] = mm(h["t"], h["beta"] * h["r"])
    for h in heads:
        h["dp"] = jnp.where(row >= col, mm(h["go"], h["u"], NT), 0.0)
    for h in heads:
        dqp = mm(h["go"], h["s"], NT) + mm(h["dp"], h["km"])
        h["dq"] = unit_back(dqp * h["plus"], h["qn"], h["q_scale"])
        h["dcum"] = dqp * h["qp"]
        h["dkm"] = mm(h["dp"], h["qp"], TN)
    return heads


def back_heads(heads):
    size = heads[0]["k"].shape[0]
    row, col = iotas(size)
    ones = jnp.where(row <= col, 1.0, 0.0).astype(BF16)
    for h in heads:
        kn, k_scale = unit(h["k"].astype(F32))
        cum = h["cum"]
        plus, minus, end = jnp.exp(cum), jnp.exp(-cum), jnp.exp(cum[-1:] - cum)
        h.update(kn=kn, k_scale=k_scale, plus=plus, minus=minus, end=end, kp=kn * plus)
        h["w"] = h["wb"] + mm(h["wa"], h["x"])
    for h in heads:
        h["dv"] = h["beta"] * h["w"]
        h["dm"] = jnp.where(row > col, -mm(h["w"], h["u"], NT), 0.0)
        h["dke"] = mm(h["u"], h["x"], NT)
    for h in heads:
        kn = h["kn"]
        km, ke = kn * h["minus"], kn * h["end"]
        dmb = h["beta"] * h["dm"]
        h["dbeta"] = jnp.sum(h["w"] * h["r"] + h["dm"] * h["kk"], axis=1, keepdims=True)
        dkp = mm(dmb, km) - mm(h["dv"], h["s"], NT)
        dkm = mm(dmb, h["kp"], TN) + h["dkm"]
        ended = h["dke"] * ke
        kept = jnp.sum((h["x"] * h["s"]).T, axis=0, keepdims=True) * jnp.exp(h["cum"][-1:])
        last = jnp.sum(ended, axis=0, keepdims=True) + kept
        dcum = h["dcum"] + dkp * h["kp"] - dkm * km - ended
        h["dg"] = sum_by(ones, dcum) + last
        grad = dkp * h["plus"] + dkm * h["minus"] + h["dke"] * h["end"]
        h["dk"] = unit_back(grad, kn, h["k_scale"])
    for h in heads:
        gate = sigmoid(h["gate_in"])
        h["dgate"] = h["dg"] * -h["rate"] * gate
        h["rate_row"] = -jnp.sum(h["dg"] * softplus(h["gate_in"]), axis=0, keepdims=True)
        h["bias_row"] = jnp.sum(h["dgate"], axis=0, keepdims=True)
    return heads


def column(table, index):
    lanes = lax.broadcasted_iota(jnp.int32, table.shape, 1)
    return jnp.sum(jnp.where(lanes == index, table, 0.0), axis=1, keepdims=True)


def fused_kernel(
    shards, count_ctx, group,
    hidden_in, q_in, k_in, v_in, go_in, s_in, down_in, up_in, beta_in, bias_in, rate_in,
    dq_out, dk_out, dv_out, dhidden_out, out,
    bias, rate, hidden, q, k, v, go, s, dq, dk, dv, dhidden, down_all, up_all, beta_all, beta_full,
    low, gates, cum, t, wa, wb, u, r, kk, dcum, dkm, maps, adds, sent, got,
    low_sum, beta_cot, rows, packed,
    core_got, core_sum, chip_got, chip_sum, piece_got, total, spread,
    load_sem, store_sem, gather_send, gather_recv, chain_send, chain_recv,
    core_send, core_recv, chip_send, chip_recv, piece_send, piece_recv, spread_send, spread_recv,
):
    me, mine = lax.axis_index("fsdp"), lax.axis_index("ctx")
    chips = shards // 2
    chip, core = me // 2, me % 2
    sibling = chip * 2 + (1 - core)
    peers = [lax.rem(chip + d, chips) * 2 + core for d in range(1, chips)]
    sources = [lax.rem(chip + chips - d, chips) * 2 + core for d in range(1, chips)]
    piece = packed.shape[1] // count_ctx
    count, size = s.shape[0], s.shape[-1]
    groups = count // group
    per_shard = count // shards
    deep = down_all.shape[1]
    first_rep = deep + per_shard * size

    own = [(down_in, down_all.at[me]), (beta_in, beta_all.at[me])]
    own += [
        (up_in.at[:, pl.ds(i * size, size)], up_all.at[me, i]) for i in range(per_shard)
    ]
    rest_in = [(hidden_in, hidden), (bias_in, bias), (rate_in, rate), (k_in, k)]
    rest_in += [(q_in, q), (go_in, go), (s_in, s), (v_in, v)]
    loads = [
        pltpu.make_async_copy(src, dst, load_sem.at[i]) for i, (src, dst) in enumerate(own + rest_in)
    ]
    for c in loads:
        c.start()
    barrier = pltpu.get_barrier_semaphore()
    for other in [sibling] + peers:
        pl.semaphore_signal(barrier, inc=1, device_id={"fsdp": other}, device_id_type=MESH)

    def greet(d, _):
        pl.semaphore_signal(
            barrier, inc=1, device_id={"ctx": lax.rem(mine + d, count_ctx)}, device_id_type=MESH
        )
        return 0

    lax.fori_loop(1, count_ctx, greet, 0)
    low_sum[...] = jnp.zeros_like(low_sum)
    beta_cot[...] = jnp.zeros_like(beta_cot)

    @pl.when(mine == count_ctx - 1)
    def _():
        got[...] = jnp.zeros_like(got)

    for c in loads[: len(own)]:
        c.wait()
    pl.semaphore_wait(barrier, chips + count_ctx - 1)

    def weights(shard, target, slot, i):
        ref = (down_all, beta_all, up_all)[i]
        return pltpu.make_async_remote_copy(
            src_ref=ref.at[shard], dst_ref=ref.at[shard],
            send_sem=gather_send.at[slot, i], recv_sem=gather_recv.at[slot, i],
            device_id={"fsdp": target}, device_id_type=MESH,
        )

    def send_own(pieces):
        for i in pieces:
            for d, peer in enumerate(peers):
                weights(me, peer, 1 + d, i).start()
        for i in pieces:
            weights(me, sibling, 0, i).start()

    def pass_on(pieces):
        for i in pieces:
            for d, source in enumerate(sources):
                weights(source, peers[d], 1 + d, i).wait_recv()
                weights(source, sibling, chips + d, i).start()
        for i in pieces:
            weights(sibling, sibling, 0, i).wait_recv()

    def take_passed(pieces, d):
        theirs = (sources[d] // 2) * 2 + (1 - core)
        for i in pieces:
            weights(theirs, sibling, chips + d, i).wait_recv()

    send_own((0, 1, 2))
    pass_on((0, 1))
    for d in range(chips - 1):
        take_passed((0, 1), d)
    by_shard = groups == shards
    if not by_shard:
        pass_on((2,))
        for d in range(chips - 1):
            take_passed((2,), d)
    for c in loads[len(own) :]:
        c.wait()

    def order(i):
        if not by_shard:
            return i
        return lax.rem(chip + i // 2, chips) * 2 + lax.rem(core + i, 2)

    def up_ready(i):
        if not by_shard:
            return

        @pl.when(i == 1)
        def _():
            pass_on((2,))

        for d in range(chips - 1):

            @pl.when(i == 2 * (chips - 1 - d) + 1)
            def _():
                take_passed((2,), d)

    for shard in range(shards):
        turned = beta_all[shard].astype(F32).T
        beta_full[shard * deep : (shard + 1) * deep, :] = turned[:deep].astype(BF16)
    low[...] = dot(hidden[...], down_all[...].reshape(shards * deep, -1)).astype(BF16)
    gates[...] = sigmoid(dot(hidden[...], beta_full[...]))

    def chain_copy(head):
        return pltpu.make_async_remote_copy(
            src_ref=sent.at[head], dst_ref=got.at[head],
            send_sem=chain_send.at[head], recv_sem=chain_recv.at[head],
            device_id={"ctx": jnp.maximum(mine - 1, 0)}, device_id_type=MESH,
        )

    hop = count_ctx - 1 - mine
    late = jnp.minimum(groups + 1 + 2 * (hop - groups), 2 * groups - 1)
    first_slot = jnp.where(hop < groups, hop, late)

    def chain_turn(head, _):
        @pl.when(mine < count_ctx - 1)
        def _():
            chain_copy(head).wait_recv()

        @pl.when(mine > 0)
        def _():
            value = got[head]
            both = jnp.concatenate([value, value], axis=0)
            sent[head] = (adds[head] + dot(maps[head], both)).astype(BF16)
            chain_copy(head).start()

        return 0

    def chain(slot):
        part = slot - first_slot

        @pl.when((part >= 0) & (part < groups))
        def _():
            at = order(part) * group
            lax.fori_loop(at, at + group, chain_turn, 0)

    def take(g, i):
        head = g * group + i
        at = pl.ds(pl.multiple_of(head * size, size), size)
        return head, at, dict(rate=rate[:, at], beta=column(gates[...], head))

    def gate_in(head, at):
        return dot(low[...], up_all[head // per_shard, head % per_shard]) + bias[:, at]

    def first(turn, _):
        up_ready(turn)
        g = order(turn)
        heads = []
        for i in range(group):
            head, at, h = take(g, i)
            h.update(q=q[:, at], k=k[:, at], go=go[:, at], gate_in=gate_in(head, at))
            heads.append(h)
        for i, h in enumerate(first_heads(heads)):
            n = g * group + i
            cum[n], kk[n], t[n], wa[n], wb[n] = h["cum"], h["kk"], h["t"], h["wa"].astype(BF16), h["wb"]
            maps[n], adds[n] = jnp.concatenate(halves(h["map"]), axis=1), h["add"]
        chain(turn)
        return 0

    def rest(turn, _):
        g = order(turn)
        heads = []
        for i in range(group):
            head, at, h = take(g, i)
            h.update(q=q[:, at], k=k[:, at], v=v[:, at], go=go[:, at])
            h.update(s=s[head], cum=cum[head], t=t[head])
            heads.append(h)
        for i, h in enumerate(rest_heads(heads)):
            n, at, _ = take(g, i)
            dq[:, at] = h["dq"].astype(BF16)
            u[n], r[n], dcum[n], dkm[n] = h["u"].astype(BF16), h["r"], h["dcum"], h["dkm"]
        chain(groups + turn)
        return 0

    lanes = lax.broadcasted_iota(jnp.int32, beta_cot.shape, 1)

    def back(turn, _):
        g = order(turn)
        heads = []
        for i in range(group):
            n, at, h = take(g, i)
            h.update(k=k[:, at], s=s[n], x=got[n].astype(F32), gate_in=gate_in(n, at))
            h.update(cum=cum[n], wa=wa[n], wb=wb[n], u=u[n], r=r[n], kk=kk[n], dcum=dcum[n], dkm=dkm[n])
            heads.append(h)
        for i, h in enumerate(back_heads(heads)):
            head, at, _ = take(g, i)
            dk[:, at] = h["dk"].astype(BF16)
            dv[:, at] = h["dv"].astype(BF16)
            half = h["dgate"].astype(BF16)
            place = pl.multiple_of(deep + (head % per_shard) * size, 16)
            packed[head // per_shard, pl.ds(place, size), :] = dot(low[...], half, TN).astype(BF16)
            low_sum[...] += dot(half, up_all[head // per_shard, head % per_shard], NT)
            beta_cot[...] += jnp.where(lanes == head, h["dbeta"], 0.0)
            rows[pl.ds(head, 1), :] = h["bias_row"]
            rows[pl.ds(count + head, 1), :] = h["rate_row"]
        chain(2 * groups + turn)
        return 0

    stores = [
        pltpu.make_async_copy(src, dst, store_sem.at[i])
        for i, (src, dst) in enumerate(
            ((dq, dq_out), (dk, dk_out), (dv, dv_out), (dhidden, dhidden_out))
        )
    ]
    lax.fori_loop(0, groups, first, 0)
    lax.fori_loop(0, groups, rest, 0)
    stores[0].start()
    lax.fori_loop(0, groups, back, 0)
    stores[1].start()
    stores[2].start()

    low_grad = low_sum[...].astype(BF16)
    gate = gates[...]
    score = (beta_cot[...] * gate * (1.0 - gate)).astype(BF16)
    down_term = dot(hidden[...], low_grad, TN).astype(BF16)
    beta_term = dot(score, hidden[...], TN).astype(BF16)
    tail = rows[...].astype(BF16)
    blocks = hidden.shape[1] // size
    for shard in range(shards):
        packed[shard, :deep, :] = down_term[shard * deep : (shard + 1) * deep]
        for b in range(blocks):
            place = first_rep + b * count
            packed[shard, place : place + count, :] = beta_term[:, b * size : (b + 1) * size]
        place = first_rep + blocks * count
        packed[shard, place : place + 2 * count, :] = tail
        if place + 2 * count < packed.shape[1]:
            left = packed.shape[1] - place - 2 * count
            packed[shard, place + 2 * count :, :] = jnp.zeros((left, packed.shape[2]), BF16)

    def core_copy(c):
        return pltpu.make_async_remote_copy(
            src_ref=packed.at[c * 2 + (1 - core)], dst_ref=core_got.at[c],
            send_sem=core_send.at[c], recv_sem=core_recv.at[c],
            device_id={"fsdp": sibling}, device_id_type=MESH,
        )

    def chip_copy(d, peer):
        return pltpu.make_async_remote_copy(
            src_ref=core_sum.at[peer // 2], dst_ref=chip_got.at[d],
            send_sem=chip_send.at[d], recv_sem=chip_recv.at[d],
            device_id={"fsdp": peer}, device_id_type=MESH,
        )

    order = [peer // 2 for peer in peers] + [chip]
    for c in order:
        core_copy(c).start()
    dhidden[...] = (
        dot(low_grad, down_all[...].reshape(shards * deep, -1), NT) + dot(score, beta_full[...], NT)
    ).astype(BF16)
    stores[3].start()
    for d, c in enumerate(order):
        core_copy(c).wait_recv()
        both = packed[c * 2 + core].astype(F32) + core_got[c].astype(F32)
        if d < chips - 1:
            core_sum[c] = both.astype(BF16)
            chip_copy(d, peers[d]).start()
        else:
            own = both
    for d in range(chips - 1):
        chip_copy(d, peers[d]).wait_recv()
        own = own + chip_got[d].astype(F32)
    chip_sum[...] = own.astype(BF16)

    def piece_copy(d):
        other = lax.rem(mine + d, count_ctx)
        at = pl.multiple_of(other * piece, 16)
        return pltpu.make_async_remote_copy(
            src_ref=chip_sum.at[pl.ds(at, piece)], dst_ref=piece_got.at[d - 1],
            send_sem=piece_send.at[d - 1], recv_sem=piece_recv.at[d - 1],
            device_id={"ctx": other}, device_id_type=MESH,
        )

    def spread_copy(d):
        return pltpu.make_async_remote_copy(
            src_ref=total, dst_ref=spread.at[d - 1],
            send_sem=spread_send.at[d - 1], recv_sem=spread_recv.at[d - 1],
            device_id={"ctx": lax.rem(mine + d, count_ctx)}, device_id_type=MESH,
        )

    def start_piece(d, _):
        piece_copy(d).start()
        return 0

    def add_piece(d, so_far):
        piece_copy(d).wait_recv()
        return so_far + piece_got[d - 1].astype(F32)

    def start_spread(d, _):
        spread_copy(d).start()
        return 0

    def place_spread(d, _):
        spread_copy(d).wait_recv()
        source = lax.rem(mine + count_ctx - d, count_ctx)
        out[pl.ds(pl.multiple_of(source * piece, 16), piece), :] = spread[d - 1].astype(F32)
        return 0

    def finish(d, _):
        piece_copy(d).wait_send()
        spread_copy(d).wait_send()
        return 0

    lax.fori_loop(1, count_ctx, start_piece, 0)
    at = pl.multiple_of(mine * piece, 16)
    summed = lax.fori_loop(1, count_ctx, add_piece, chip_sum[pl.ds(at, piece), :].astype(F32))
    total[...] = summed.astype(BF16)
    lax.fori_loop(1, count_ctx, start_spread, 0)
    out[pl.ds(at, piece), :] = total[...].astype(F32)
    lax.fori_loop(1, count_ctx, place_spread, 0)
    lax.fori_loop(1, count_ctx, finish, 0)
    for c in range(chips):
        core_copy(c).wait_send()
    for d, peer in enumerate(peers):
        chip_copy(d, peer).wait_send()
    for slot in range(2 * chips - 1):
        for i in range(3):
            weights(me, sibling, slot, i).wait_send()

    @pl.when(mine > 0)
    def _():
        def done(head, _):
            chain_copy(head).wait_send()
            return 0

        lax.fori_loop(0, count, done, 0)

    for c in stores:
        c.wait()


def place_kernel(
    deep, per_shard, vectors_at,
    dq, dk, dv, dhidden, summed, dq_out, dk_out, dv_out, dhidden_out, down, up, bias, rate, sem,
):
    count, size = bias.shape
    pairs = [(dq, dq_out), (dk, dk_out), (dv, dv_out), (dhidden, dhidden_out)]
    pairs += [(summed.at[pl.ds(0, deep)], down)]
    rank = up.shape[0]
    pairs += [
        (summed.at[pl.ds(deep + i * rank, rank)], up.at[:, pl.ds(i * size, size)])
        for i in range(per_shard)
    ]
    pairs += [(summed.at[pl.ds(vectors_at, count)], bias)]
    pairs += [(summed.at[pl.ds(vectors_at + count, count)], rate)]
    copies = [pltpu.make_async_copy(src, dst, sem.at[i]) for i, (src, dst) in enumerate(pairs)]
    for c in copies:
        c.start()
    for c in copies:
        c.wait()


def remote(collective):
    return pltpu.CompilerParams(
        collective_id=collective, has_side_effects=True, vmem_limit_bytes=VMEM_LIMIT
    )


def on_device(
    shards, blocks_ctx,
    hidden, query_heads, key_heads, value_heads, out_grad, checkpoint,
    gate_down, gate_up, gate_bias, decay_rate, beta_weight,
):
    tokens, width = hidden.shape[1], hidden.shape[2]
    count, size = checkpoint.shape[2], checkpoint.shape[3]
    rank = gate_down.shape[1]
    deep = gate_down.shape[0]
    per_shard = count // shards
    chips = shards // 2
    hidden, q, k, v, go = (a[0] for a in (hidden, query_heads, key_heads, value_heads, out_grad))
    state = checkpoint[0, 0]
    bias, rate = gate_bias.reshape(1, -1), decay_rate.reshape(1, -1)
    dma = pltpu.SemaphoreType.DMA

    group = 4 if count % 4 == 0 else 1
    rows = deep + per_shard * size + (width // size) * count + 2 * count
    unit_size = 16 * blocks_ctx
    rows = -(-rows // unit_size) * unit_size
    piece = rows // blocks_ctx
    far = max(chips - 1, 1)
    wide = -(-deep // size) * size
    beta_t = jnp.pad(beta_weight.T, ((0, 0), (0, wide - deep)))
    channels = count * size
    anywhere = pl.BlockSpec(memory_space=pl.ANY)
    heads_f32 = pltpu.VMEM((count, tokens, size), F32)
    heads_bf16 = pltpu.VMEM((count, tokens, size), BF16)
    states_f32 = pltpu.VMEM((count, size, size), F32)
    states_bf16 = pltpu.VMEM((count, size, size), BF16)
    mixed = pltpu.VMEM((count, tokens, tokens), F32)
    sided = pltpu.VMEM((tokens, channels), BF16)
    sized = pltpu.VMEM((tokens, width), BF16)
    dq, dk, dv, dhidden, summed = pl.pallas_call(
        functools.partial(fused_kernel, shards, blocks_ctx, group),
        out_shape=(
            jax.ShapeDtypeStruct((tokens, channels), BF16),
            jax.ShapeDtypeStruct((tokens, channels), BF16),
            jax.ShapeDtypeStruct((tokens, channels), BF16),
            jax.ShapeDtypeStruct((tokens, width), BF16),
            jax.ShapeDtypeStruct((rows, size), F32),
        ),
        in_specs=[anywhere] * 11,
        out_specs=(anywhere,) * 4 + (pl.BlockSpec(memory_space=pltpu.VMEM),),
        scratch_shapes=[
            pltpu.VMEM((1, channels), F32), pltpu.VMEM((1, channels), F32),
            sized, sided, sided, sided, sided, states_f32, sided, sided, sided, sized,
            pltpu.VMEM((shards, deep, rank), BF16),
            pltpu.VMEM((shards, per_shard, rank, size), BF16),
            pltpu.VMEM((shards, count, wide), BF16), pltpu.VMEM((width, count), BF16),
            pltpu.VMEM((tokens, rank), BF16), pltpu.VMEM((tokens, count), F32),
            heads_f32, mixed, heads_bf16, heads_f32, heads_bf16, heads_f32, mixed, heads_f32, heads_f32,
            pltpu.VMEM((count, size, 2 * size), BF16), states_f32, states_bf16, states_bf16,
            pltpu.VMEM((tokens, rank), F32), pltpu.VMEM((tokens, count), F32),
            pltpu.VMEM((2 * count, size), F32), pltpu.VMEM((shards, rows, size), BF16),
            pltpu.VMEM((chips, rows, size), BF16), pltpu.VMEM((chips, rows, size), BF16),
            pltpu.VMEM((far, rows, size), BF16), pltpu.VMEM((rows, size), BF16),
            pltpu.VMEM((blocks_ctx - 1, piece, size), BF16), pltpu.VMEM((piece, size), BF16),
            pltpu.VMEM((blocks_ctx - 1, piece, size), BF16),
            dma((10 + per_shard,)), dma((4,)), dma((2 * chips - 1, 3)), dma((2 * chips - 1, 3)),
            dma((count,)), dma((count,)),
            dma((chips,)), dma((chips,)), dma((far,)), dma((far,)),
            dma((blocks_ctx - 1,)), dma((blocks_ctx - 1,)),
            dma((blocks_ctx - 1,)), dma((blocks_ctx - 1,)),
        ],
        compiler_params=remote(0),
        name="delta_backward",
    )(hidden, q, k, v, go, state, gate_down, gate_up, beta_t, bias, rate)

    up_at = deep + per_shard * size
    beta_at = up_at + (width // size) * count
    flat = jax.ShapeDtypeStruct((count, size), F32)
    dq, dk, dv, dhidden, down_grad, up_grad, bias_grad, rate_grad = pl.pallas_call(
        functools.partial(place_kernel, deep, per_shard, beta_at),
        out_shape=(
            jax.ShapeDtypeStruct((tokens, channels), BF16),
            jax.ShapeDtypeStruct((tokens, channels), BF16),
            jax.ShapeDtypeStruct((tokens, channels), BF16),
            jax.ShapeDtypeStruct((tokens, width), BF16),
            jax.ShapeDtypeStruct((deep, rank), F32),
            jax.ShapeDtypeStruct((rank, per_shard * size), F32),
            flat, flat,
        ),
        in_specs=[anywhere] * 5,
        out_specs=(anywhere,) * 8,
        scratch_shapes=[dma((7 + per_shard,))],
        compiler_params=pltpu.CompilerParams(vmem_limit_bytes=VMEM_LIMIT),
        name="place_results",
    )(dq, dk, dv, dhidden, summed)
    beta_rows = summed[up_at:beta_at].reshape(width // size, count, size)
    beta_full = beta_rows.swapaxes(1, 2).reshape(width, count)
    beta_grad = lax.dynamic_slice_in_dim(beta_full, lax.axis_index("fsdp") * deep, deep, 0)
    return (
        dq[None], dk[None], dv[None], dhidden[None],
        down_grad, up_grad, beta_grad, bias_grad.reshape(-1), rate_grad.reshape(-1),
    )


def solution(mesh):
    shards, blocks_ctx = mesh.shape["fsdp"], mesh.shape["ctx"]
    tokens, state = P("fsdp", "ctx", None), P("fsdp", "ctx", None, None, None)
    by_row, by_col = P("fsdp", None), P(None, "fsdp")
    return jax.shard_map(
        functools.partial(on_device, shards, blocks_ctx),
        mesh=mesh,
        in_specs=(tokens,) * 5 + (state, by_row, by_col, P(), P(), by_row),
        out_specs=(tokens,) * 4 + (by_row, by_col, by_row, P(), P()),
        check_vma=False,
    )
```

```python
import functools

import jax
import jax.numpy as jnp
from jax import lax
from jax.experimental import pallas as pl
from jax.experimental.pallas import tpu as pltpu
from jax.sharding import PartitionSpec as P

EPSILON = 1e-06
MESH = pl.DeviceIdType.MESH
F32, BF16 = jnp.float32, jnp.bfloat16
VMEM_LIMIT = 60 * 1024 * 1024
NN, NT, TN = ((1,), (0,)), ((1,), (1,)), ((0,), (0,))
INV_PASSES = 1
PASSES = 3


def dot(left, right, dims=NN):
    return lax.dot_general(left, right, (dims, ((), ())), preferred_element_type=F32)


def halves(value):
    if value.dtype == BF16:
        return value, None
    high = value.astype(BF16)
    return high, (value - high.astype(F32)).astype(BF16)


def mm(left, right, dims=NN, passes=None):
    passes = PASSES if passes is None else passes
    if passes == 1:
        return dot(left.astype(BF16), right.astype(BF16), dims)
    left_high, left_low = halves(left)
    right_high, right_low = halves(right)
    lefts, rights = [left_high], [right_high]
    if left_low is not None:
        lefts, rights = lefts + [left_low], rights + [right_high]
    if right_low is not None:
        lefts, rights = lefts + [left_high], rights + [right_low]
    return dot(
        jnp.concatenate(lefts, axis=dims[0][0]), jnp.concatenate(rights, axis=dims[1][0]), dims
    )


def sum_by(ones, value):
    high = value.astype(BF16)
    rest = value - high.astype(F32)
    mid = rest.astype(BF16)
    low = (rest - mid.astype(F32)).astype(BF16)
    return dot(jnp.concatenate([ones] * 3, axis=1), jnp.concatenate([high, mid, low], axis=0))


def iotas(size):
    return (
        lax.broadcasted_iota(jnp.int32, (size, size), 0),
        lax.broadcasted_iota(jnp.int32, (size, size), 1),
    )


def inverse(systems):
    size = systems[0].shape[0]
    row, col = iotas(size)
    eye = jnp.where(row == col, 1.0, 0.0)

    def off(block):
        same = row // (2 * block) == col // (2 * block)
        return same & ((row // block) % 2 == 1) & ((col // block) % 2 == 0)

    found = [eye - jnp.where(off(1), system, 0.0) for system in systems]
    block = 2
    while block < size:
        mask = off(block)
        parts = [mm(jnp.where(mask, s, 0.0), t, NN, INV_PASSES) for s, t in zip(systems, found)]
        found = [t - mm(t, p, NN, INV_PASSES) for t, p in zip(found, parts)]
        block *= 2
    return found


def softplus(value):
    return jnp.maximum(value, 0.0) + jnp.log1p(jnp.exp(-jnp.abs(value)))


def sigmoid(value):
    return 1.0 / (1.0 + jnp.exp(-value))


def unit(rows):
    scale = lax.rsqrt(jnp.sum(rows * rows, axis=-1, keepdims=True) + EPSILON)
    return rows * scale, scale


def unit_back(grad, rows, scale):
    return scale * (grad - rows * jnp.sum(grad * rows, axis=-1, keepdims=True))


def head_terms(keys, gate_in, rate):
    size = keys.shape[0]
    row, col = iotas(size)
    kn, k_scale = unit(keys.astype(F32))
    ones = jnp.where(row >= col, 1.0, 0.0).astype(BF16)
    cumulative = sum_by(ones, -rate * softplus(gate_in))
    return kn, k_scale, cumulative


def first_heads(heads):
    row, col = iotas(heads[0]["k"].shape[0])
    for h in heads:
        kn, _, cum = head_terms(h["k"], h["gate_in"], h["rate"])
        qn, _ = unit(h["q"].astype(F32))
        plus = jnp.exp(cum)
        h.update(cum=cum, kp=kn * plus, km=kn * jnp.exp(-cum), qp=qn * plus)
        h.update(ke=kn * jnp.exp(cum[-1:] - cum))
    for h in heads:
        h["kk"] = jnp.where(row > col, mm(h["kp"], h["km"], NT), 0.0)
        h["p"] = jnp.where(row >= col, mm(h["qp"], h["km"], NT), 0.0)
    for h, t in zip(heads, inverse([h["kk"] * h["beta"] for h in heads])):
        h["t"] = t
    for h in heads:
        h["pg"] = mm(h["p"], h["go"], TN)
    for h in heads:
        h["wa"] = mm(h["t"], h["ke"], TN)
        h["wb"] = mm(h["t"], h["pg"], TN)
    for h in heads:
        kb = h["kp"] * h["beta"]
        end = jnp.exp(h["cum"][-1:])
        h["map"] = jnp.where(row == col, end, 0.0) - mm(kb, h["wa"], TN)
        h["add"] = mm(h["qp"], h["go"], TN) - mm(kb, h["wb"], TN)
    return heads


def rest_heads(heads):
    row, col = iotas(heads[0]["k"].shape[0])
    for h in heads:
        kn, _ = unit(h["k"].astype(F32))
        qn, q_scale = unit(h["q"].astype(F32))
        plus = jnp.exp(h["cum"])
        h.update(plus=plus, qn=qn, q_scale=q_scale)
        h.update(kp=kn * plus, km=kn * jnp.exp(-h["cum"]), qp=qn * plus)
        h["r"] = h["v"].astype(F32) - mm(h["kp"], h["s"])
    for h in heads:
        h["u"] = mm(h["t"], h["beta"] * h["r"])
    for h in heads:
        h["dp"] = jnp.where(row >= col, mm(h["go"], h["u"], NT), 0.0)
    for h in heads:
        dqp = mm(h["go"], h["s"], NT) + mm(h["dp"], h["km"])
        h["dq"] = unit_back(dqp * h["plus"], h["qn"], h["q_scale"])
        h["dcum"] = dqp * h["qp"]
        h["dkm"] = mm(h["dp"], h["qp"], TN)
    return heads


def back_heads(heads):
    size = heads[0]["k"].shape[0]
    row, col = iotas(size)
    ones = jnp.where(row <= col, 1.0, 0.0).astype(BF16)
    for h in heads:
        kn, k_scale = unit(h["k"].astype(F32))
        cum = h["cum"]
        plus, minus, end = jnp.exp(cum), jnp.exp(-cum), jnp.exp(cum[-1:] - cum)
        h.update(kn=kn, k_scale=k_scale, plus=plus, minus=minus, end=end, kp=kn * plus)
        h["w"] = h["wb"] + mm(h["wa"], h["x"])
    for h in heads:
        h["dv"] = h["beta"] * h["w"]
        h["dm"] = jnp.where(row > col, -mm(h["w"], h["u"], NT), 0.0)
        h["dke"] = mm(h["u"], h["x"], NT)
    for h in heads:
        kn = h["kn"]
        km, ke = kn * h["minus"], kn * h["end"]
        dmb = h["beta"] * h["dm"]
        h["dbeta"] = jnp.sum(h["w"] * h["r"] + h["dm"] * h["kk"], axis=1, keepdims=True)
        dkp = mm(dmb, km) - mm(h["dv"], h["s"], NT)
        dkm = mm(dmb, h["kp"], TN) + h["dkm"]
        ended = h["dke"] * ke
        kept = jnp.sum((h["x"] * h["s"]).T, axis=0, keepdims=True) * jnp.exp(h["cum"][-1:])
        last = jnp.sum(ended, axis=0, keepdims=True) + kept
        dcum = h["dcum"] + dkp * h["kp"] - dkm * km - ended
        h["dg"] = sum_by(ones, dcum) + last
        grad = dkp * h["plus"] + dkm * h["minus"] + h["dke"] * h["end"]
        h["dk"] = unit_back(grad, kn, h["k_scale"])
    for h in heads:
        gate = sigmoid(h["gate_in"])
        h["dgate"] = h["dg"] * -h["rate"] * gate
        h["rate_row"] = -jnp.sum(h["dg"] * softplus(h["gate_in"]), axis=0, keepdims=True)
        h["bias_row"] = jnp.sum(h["dgate"], axis=0, keepdims=True)
    return heads


def column(table, index):
    lanes = lax.broadcasted_iota(jnp.int32, table.shape, 1)
    return jnp.sum(jnp.where(lanes == index, table, 0.0), axis=1, keepdims=True)


def fused_kernel(
    shards, count_ctx, group,
    hidden_in, q_in, k_in, v_in, go_in, s_in, down_in, up_in, beta_in, bias_in, rate_in,
    dq_out, dk_out, dv_out, dhidden_out, out,
    bias, rate, hidden, q, k, v, go, s, dq, dk, dv, dhidden, down_all, up_all, beta_all, beta_full,
    low, gates, cum, t, wa, wb, u, r, kk, dcum, dkm, maps, adds, sent, got,
    low_sum, beta_cot, rows, packed,
    core_got, core_sum, chip_got, chip_sum, piece_got, total, spread,
    load_sem, store_sem, gather_send, gather_recv, chain_send, chain_recv,
    core_send, core_recv, chip_send, chip_recv, piece_send, piece_recv, spread_send, spread_recv,
):
    me, mine = lax.axis_index("fsdp"), lax.axis_index("ctx")
    chips = shards // 2
    chip, core = me // 2, me % 2
    sibling = chip * 2 + (1 - core)
    peers = [lax.rem(chip + d, chips) * 2 + core for d in range(1, chips)]
    sources = [lax.rem(chip + chips - d, chips) * 2 + core for d in range(1, chips)]
    piece = packed.shape[1] // count_ctx
    count, size = s.shape[0], s.shape[-1]
    groups = count // group
    per_shard = count // shards
    deep = down_all.shape[1]
    first_rep = deep + per_shard * size

    own = [(down_in, down_all.at[me]), (beta_in, beta_all.at[me])]
    own += [
        (up_in.at[:, pl.ds(i * size, size)], up_all.at[me, i]) for i in range(per_shard)
    ]
    rest_in = [(hidden_in, hidden), (bias_in, bias), (rate_in, rate), (k_in, k)]
    rest_in += [(q_in, q), (go_in, go), (s_in, s), (v_in, v)]
    loads = [
        pltpu.make_async_copy(src, dst, load_sem.at[i]) for i, (src, dst) in enumerate(own + rest_in)
    ]
    for c in loads:
        c.start()
    barrier = pltpu.get_barrier_semaphore()
    for other in [sibling] + peers:
        pl.semaphore_signal(barrier, inc=1, device_id={"fsdp": other}, device_id_type=MESH)

    def greet(d, _):
        pl.semaphore_signal(
            barrier, inc=1, device_id={"ctx": lax.rem(mine + d, count_ctx)}, device_id_type=MESH
        )
        return 0

    lax.fori_loop(1, count_ctx, greet, 0)
    low_sum[...] = jnp.zeros_like(low_sum)
    beta_cot[...] = jnp.zeros_like(beta_cot)

    @pl.when(mine == count_ctx - 1)
    def _():
        got[...] = jnp.zeros_like(got)

    for c in loads[: len(own)]:
        c.wait()
    pl.semaphore_wait(barrier, chips + count_ctx - 1)

    def weights(shard, target, slot, i):
        ref = (down_all, beta_all, up_all)[i]
        return pltpu.make_async_remote_copy(
            src_ref=ref.at[shard], dst_ref=ref.at[shard],
            send_sem=gather_send.at[slot, i], recv_sem=gather_recv.at[slot, i],
            device_id={"fsdp": target}, device_id_type=MESH,
        )

    def send_own(pieces):
        for i in pieces:
            for d, peer in enumerate(peers):
                weights(me, peer, 1 + d, i).start()
        for i in pieces:
            weights(me, sibling, 0, i).start()

    def pass_on(pieces):
        for i in pieces:
            for d, source in enumerate(sources):
                weights(source, peers[d], 1 + d, i).wait_recv()
                weights(source, sibling, chips + d, i).start()
        for i in pieces:
            weights(sibling, sibling, 0, i).wait_recv()

    def take_passed(pieces, d):
        theirs = (sources[d] // 2) * 2 + (1 - core)
        for i in pieces:
            weights(theirs, sibling, chips + d, i).wait_recv()

    send_own((0, 1, 2))
    pass_on((0, 1))
    for d in range(chips - 1):
        take_passed((0, 1), d)
    by_shard = groups == shards
    if not by_shard:
        pass_on((2,))
        for d in range(chips - 1):
            take_passed((2,), d)
    for c in loads[len(own) :]:
        c.wait()

    def order(i):
        if not by_shard:
            return i
        return lax.rem(chip + i // 2, chips) * 2 + lax.rem(core + i, 2)

    def up_ready(i):
        if not by_shard:
            return

        @pl.when(i == 1)
        def _():
            pass_on((2,))

        for d in range(chips - 1):

            @pl.when(i == 2 * (chips - 1 - d) + 1)
            def _():
                take_passed((2,), d)

    for shard in range(shards):
        turned = beta_all[shard].astype(F32).T
        beta_full[shard * deep : (shard + 1) * deep, :] = turned.astype(BF16)
    low[...] = dot(hidden[...], down_all[...].reshape(shards * deep, -1)).astype(BF16)
    gates[...] = sigmoid(dot(hidden[...], beta_full[...]))

    def chain_copy(head):
        return pltpu.make_async_remote_copy(
            src_ref=sent.at[head], dst_ref=got.at[head],
            send_sem=chain_send.at[head], recv_sem=chain_recv.at[head],
            device_id={"ctx": jnp.maximum(mine - 1, 0)}, device_id_type=MESH,
        )

    hop = count_ctx - 1 - mine
    late = jnp.minimum(groups + 1 + 2 * (hop - groups), 2 * groups - 1)
    first_slot = jnp.where(hop < groups, hop, late)

    def chain_turn(head, _):
        @pl.when(mine < count_ctx - 1)
        def _():
            chain_copy(head).wait_recv()

        @pl.when(mine > 0)
        def _():
            value = got[head]
            both = jnp.concatenate([value, value], axis=0)
            sent[head] = (adds[head] + dot(maps[head], both)).astype(BF16)
            chain_copy(head).start()

        return 0

    def chain(slot):
        part = slot - first_slot

        @pl.when((part >= 0) & (part < groups))
        def _():
            at = order(part) * group
            lax.fori_loop(at, at + group, chain_turn, 0)

    def take(g, i):
        head = g * group + i
        at = pl.ds(pl.multiple_of(head * size, size), size)
        return head, at, dict(rate=rate[:, at], beta=column(gates[...], head))

    def gate_in(head, at):
        return dot(low[...], up_all[head // per_shard, head % per_shard]) + bias[:, at]

    def first(turn, _):
        up_ready(turn)
        g = order(turn)
        heads = []
        for i in range(group):
            head, at, h = take(g, i)
            h.update(q=q[:, at], k=k[:, at], go=go[:, at], gate_in=gate_in(head, at))
            heads.append(h)
        for i, h in enumerate(first_heads(heads)):
            n = g * group + i
            cum[n], kk[n], t[n], wa[n], wb[n] = h["cum"], h["kk"], h["t"], h["wa"].astype(BF16), h["wb"]
            maps[n], adds[n] = jnp.concatenate(halves(h["map"]), axis=1), h["add"]
        chain(turn)
        return 0

    def rest(turn, _):
        g = order(turn)
        heads = []
        for i in range(group):
            head, at, h = take(g, i)
            h.update(q=q[:, at], k=k[:, at], v=v[:, at], go=go[:, at])
            h.update(s=s[head], cum=cum[head], t=t[head])
            heads.append(h)
        for i, h in enumerate(rest_heads(heads)):
            n, at, _ = take(g, i)
            dq[:, at] = h["dq"].astype(BF16)
            u[n], r[n], dcum[n], dkm[n] = h["u"].astype(BF16), h["r"], h["dcum"], h["dkm"]
        chain(groups + turn)
        return 0

    lanes = lax.broadcasted_iota(jnp.int32, beta_cot.shape, 1)

    def back(turn, _):
        g = order(turn)
        heads = []
        for i in range(group):
            n, at, h = take(g, i)
            h.update(k=k[:, at], s=s[n], x=got[n].astype(F32), gate_in=gate_in(n, at))
            h.update(cum=cum[n], wa=wa[n], wb=wb[n], u=u[n], r=r[n], kk=kk[n], dcum=dcum[n], dkm=dkm[n])
            heads.append(h)
        for i, h in enumerate(back_heads(heads)):
            head, at, _ = take(g, i)
            dk[:, at] = h["dk"].astype(BF16)
            dv[:, at] = h["dv"].astype(BF16)
            half = h["dgate"].astype(BF16)
            place = pl.multiple_of(deep + (head % per_shard) * size, 16)
            packed[head // per_shard, pl.ds(place, size), :] = dot(low[...], half, TN).astype(BF16)
            low_sum[...] += dot(half, up_all[head // per_shard, head % per_shard], NT)
            beta_cot[...] += jnp.where(lanes == head, h["dbeta"], 0.0)
            rows[pl.ds(head, 1), :] = h["bias_row"]
            rows[pl.ds(count + head, 1), :] = h["rate_row"]
        chain(2 * groups + turn)
        return 0

    stores = [
        pltpu.make_async_copy(src, dst, store_sem.at[i])
        for i, (src, dst) in enumerate(
            ((dq, dq_out), (dk, dk_out), (dv, dv_out), (dhidden, dhidden_out))
        )
    ]
    lax.fori_loop(0, groups, first, 0)
    lax.fori_loop(0, groups, rest, 0)
    stores[0].start()
    lax.fori_loop(0, groups, back, 0)
    stores[1].start()
    stores[2].start()

    low_grad = low_sum[...].astype(BF16)
    gate = gates[...]
    score = (beta_cot[...] * gate * (1.0 - gate)).astype(BF16)
    down_term = dot(hidden[...], low_grad, TN).astype(BF16)
    beta_term = dot(score, hidden[...], TN).astype(BF16)
    tail = rows[...].astype(BF16)
    blocks = hidden.shape[1] // size
    for shard in range(shards):
        packed[shard, :deep, :] = down_term[shard * deep : (shard + 1) * deep]
        for b in range(blocks):
            place = first_rep + b * count
            packed[shard, place : place + count, :] = beta_term[:, b * size : (b + 1) * size]
        place = first_rep + blocks * count
        packed[shard, place : place + 2 * count, :] = tail
        if place + 2 * count < packed.shape[1]:
            left = packed.shape[1] - place - 2 * count
            packed[shard, place + 2 * count :, :] = jnp.zeros((left, packed.shape[2]), BF16)

    def core_copy(c):
        return pltpu.make_async_remote_copy(
            src_ref=packed.at[c * 2 + (1 - core)], dst_ref=core_got.at[c],
            send_sem=core_send.at[c], recv_sem=core_recv.at[c],
            device_id={"fsdp": sibling}, device_id_type=MESH,
        )

    def chip_copy(d, peer):
        return pltpu.make_async_remote_copy(
            src_ref=core_sum.at[peer // 2], dst_ref=chip_got.at[d],
            send_sem=chip_send.at[d], recv_sem=chip_recv.at[d],
            device_id={"fsdp": peer}, device_id_type=MESH,
        )

    order = [peer // 2 for peer in peers] + [chip]
    for c in order:
        core_copy(c).start()
    dhidden[...] = (
        dot(low_grad, down_all[...].reshape(shards * deep, -1), NT) + dot(score, beta_full[...], NT)
    ).astype(BF16)
    stores[3].start()
    for d, c in enumerate(order):
        core_copy(c).wait_recv()
        both = packed[c * 2 + core].astype(F32) + core_got[c].astype(F32)
        if d < chips - 1:
            core_sum[c] = both.astype(BF16)
            chip_copy(d, peers[d]).start()
        else:
            own = both
    for d in range(chips - 1):
        chip_copy(d, peers[d]).wait_recv()
        own = own + chip_got[d].astype(F32)
    chip_sum[...] = own.astype(BF16)

    def piece_copy(d):
        other = lax.rem(mine + d, count_ctx)
        at = pl.multiple_of(other * piece, 16)
        return pltpu.make_async_remote_copy(
            src_ref=chip_sum.at[pl.ds(at, piece)], dst_ref=piece_got.at[d - 1],
            send_sem=piece_send.at[d - 1], recv_sem=piece_recv.at[d - 1],
            device_id={"ctx": other}, device_id_type=MESH,
        )

    def spread_copy(d):
        return pltpu.make_async_remote_copy(
            src_ref=total, dst_ref=spread.at[d - 1],
            send_sem=spread_send.at[d - 1], recv_sem=spread_recv.at[d - 1],
            device_id={"ctx": lax.rem(mine + d, count_ctx)}, device_id_type=MESH,
        )

    def start_piece(d, _):
        piece_copy(d).start()
        return 0

    def add_piece(d, so_far):
        piece_copy(d).wait_recv()
        return so_far + piece_got[d - 1].astype(F32)

    def start_spread(d, _):
        spread_copy(d).start()
        return 0

    def place_spread(d, _):
        spread_copy(d).wait_recv()
        source = lax.rem(mine + count_ctx - d, count_ctx)
        out[pl.ds(pl.multiple_of(source * piece, 16), piece), :] = spread[d - 1].astype(F32)
        return 0

    def finish(d, _):
        piece_copy(d).wait_send()
        spread_copy(d).wait_send()
        return 0

    lax.fori_loop(1, count_ctx, start_piece, 0)
    at = pl.multiple_of(mine * piece, 16)
    summed = lax.fori_loop(1, count_ctx, add_piece, chip_sum[pl.ds(at, piece), :].astype(F32))
    total[...] = summed.astype(BF16)
    lax.fori_loop(1, count_ctx, start_spread, 0)
    out[pl.ds(at, piece), :] = total[...].astype(F32)
    lax.fori_loop(1, count_ctx, place_spread, 0)
    lax.fori_loop(1, count_ctx, finish, 0)
    for c in range(chips):
        core_copy(c).wait_send()
    for d, peer in enumerate(peers):
        chip_copy(d, peer).wait_send()
    for slot in range(2 * chips - 1):
        for i in range(3):
            weights(me, sibling, slot, i).wait_send()

    @pl.when(mine > 0)
    def _():
        def done(head, _):
            chain_copy(head).wait_send()
            return 0

        lax.fori_loop(0, count, done, 0)

    for c in stores:
        c.wait()


def place_kernel(
    deep, per_shard, vectors_at,
    dq, dk, dv, dhidden, summed, dq_out, dk_out, dv_out, dhidden_out, down, up, bias, rate,
    dq_held, dk_held, dv_held, dhidden_held, held, load_sem, sem,
):
    count, size = bias.shape
    loads = [(summed, held), (dq, dq_held), (dk, dk_held), (dv, dv_held), (dhidden, dhidden_held)]
    loads = [pltpu.make_async_copy(src, dst, load_sem.at[i]) for i, (src, dst) in enumerate(loads)]
    for c in loads:
        c.start()
    pairs = [(held.at[pl.ds(0, deep)], down)]
    rank = up.shape[0]
    pairs += [
        (held.at[pl.ds(deep + i * rank, rank)], up.at[:, pl.ds(i * size, size)])
        for i in range(per_shard)
    ]
    pairs += [(held.at[pl.ds(vectors_at, count)], bias)]
    pairs += [(held.at[pl.ds(vectors_at + count, count)], rate)]
    first = len(pairs)
    pairs += [(dq_held, dq_out), (dk_held, dk_out), (dv_held, dv_out), (dhidden_held, dhidden_out)]
    copies = [pltpu.make_async_copy(src, dst, sem.at[i]) for i, (src, dst) in enumerate(pairs)]
    loads[0].wait()
    for c in copies[:first]:
        c.start()
    for load, c in zip(loads[1:], copies[first:]):
        load.wait()
        c.start()
    for c in copies:
        c.wait()


def remote(collective):
    return pltpu.CompilerParams(
        collective_id=collective, has_side_effects=True, vmem_limit_bytes=VMEM_LIMIT
    )


def on_device(
    shards, blocks_ctx,
    hidden, query_heads, key_heads, value_heads, out_grad, checkpoint,
    gate_down, gate_up, gate_bias, decay_rate, beta_weight,
):
    tokens, width = hidden.shape[1], hidden.shape[2]
    count, size = checkpoint.shape[2], checkpoint.shape[3]
    rank = gate_down.shape[1]
    deep = gate_down.shape[0]
    per_shard = count // shards
    chips = shards // 2
    hidden, q, k, v, go = (a[0] for a in (hidden, query_heads, key_heads, value_heads, out_grad))
    state = checkpoint[0, 0]
    bias, rate = gate_bias.reshape(1, -1), decay_rate.reshape(1, -1)
    dma = pltpu.SemaphoreType.DMA

    group = 4 if count % 4 == 0 else 1
    rows = deep + per_shard * size + (width // size) * count + 2 * count
    unit_size = 16 * blocks_ctx
    rows = -(-rows // unit_size) * unit_size
    piece = rows // blocks_ctx
    far = max(chips - 1, 1)
    beta_t = beta_weight.T
    channels = count * size
    anywhere = pl.BlockSpec(memory_space=pl.ANY)
    heads_f32 = pltpu.VMEM((count, tokens, size), F32)
    heads_bf16 = pltpu.VMEM((count, tokens, size), BF16)
    states_f32 = pltpu.VMEM((count, size, size), F32)
    states_bf16 = pltpu.VMEM((count, size, size), BF16)
    mixed = pltpu.VMEM((count, tokens, tokens), F32)
    sided = pltpu.VMEM((tokens, channels), BF16)
    sized = pltpu.VMEM((tokens, width), BF16)
    dq, dk, dv, dhidden, summed = pl.pallas_call(
        functools.partial(fused_kernel, shards, blocks_ctx, group),
        out_shape=(
            jax.ShapeDtypeStruct((tokens, channels), BF16),
            jax.ShapeDtypeStruct((tokens, channels), BF16),
            jax.ShapeDtypeStruct((tokens, channels), BF16),
            jax.ShapeDtypeStruct((tokens, width), BF16),
            jax.ShapeDtypeStruct((rows, size), F32),
        ),
        in_specs=[anywhere] * 11,
        out_specs=(anywhere,) * 4 + (pl.BlockSpec(memory_space=pltpu.VMEM),),
        scratch_shapes=[
            pltpu.VMEM((1, channels), F32), pltpu.VMEM((1, channels), F32),
            sized, sided, sided, sided, sided, states_f32, sided, sided, sided, sized,
            pltpu.VMEM((shards, deep, rank), BF16),
            pltpu.VMEM((shards, per_shard, rank, size), BF16),
            pltpu.VMEM((shards, count, deep), BF16), pltpu.VMEM((width, count), BF16),
            pltpu.VMEM((tokens, rank), BF16), pltpu.VMEM((tokens, count), F32),
            heads_f32, mixed, heads_bf16, heads_f32, heads_bf16, heads_f32, mixed, heads_f32, heads_f32,
            pltpu.VMEM((count, size, 2 * size), BF16), states_f32, states_bf16, states_bf16,
            pltpu.VMEM((tokens, rank), F32), pltpu.VMEM((tokens, count), F32),
            pltpu.VMEM((2 * count, size), F32), pltpu.VMEM((shards, rows, size), BF16),
            pltpu.VMEM((chips, rows, size), BF16), pltpu.VMEM((chips, rows, size), BF16),
            pltpu.VMEM((far, rows, size), BF16), pltpu.VMEM((rows, size), BF16),
            pltpu.VMEM((blocks_ctx - 1, piece, size), BF16), pltpu.VMEM((piece, size), BF16),
            pltpu.VMEM((blocks_ctx - 1, piece, size), BF16),
            dma((10 + per_shard,)), dma((4,)), dma((2 * chips - 1, 3)), dma((2 * chips - 1, 3)),
            dma((count,)), dma((count,)),
            dma((chips,)), dma((chips,)), dma((far,)), dma((far,)),
            dma((blocks_ctx - 1,)), dma((blocks_ctx - 1,)),
            dma((blocks_ctx - 1,)), dma((blocks_ctx - 1,)),
        ],
        compiler_params=remote(0),
        name="delta_backward",
    )(hidden, q, k, v, go, state, gate_down, gate_up, beta_t, bias, rate)

    up_at = deep + per_shard * size
    beta_at = up_at + (width // size) * count
    flat = jax.ShapeDtypeStruct((count, size), F32)
    dq, dk, dv, dhidden, down_grad, up_grad, bias_grad, rate_grad = pl.pallas_call(
        functools.partial(place_kernel, deep, per_shard, beta_at),
        out_shape=(
            jax.ShapeDtypeStruct((tokens, channels), BF16),
            jax.ShapeDtypeStruct((tokens, channels), BF16),
            jax.ShapeDtypeStruct((tokens, channels), BF16),
            jax.ShapeDtypeStruct((tokens, width), BF16),
            jax.ShapeDtypeStruct((deep, rank), F32),
            jax.ShapeDtypeStruct((rank, per_shard * size), F32),
            flat, flat,
        ),
        in_specs=[anywhere] * 5,
        out_specs=(anywhere,) * 8,
        scratch_shapes=[sided, sided, sided, sized, pltpu.VMEM((rows, size), F32), dma((5,)), dma((7 + per_shard,))],
        compiler_params=pltpu.CompilerParams(vmem_limit_bytes=VMEM_LIMIT),
        name="place_results",
    )(dq, dk, dv, dhidden, summed)
    beta_rows = summed[up_at:beta_at].reshape(width // size, count, size)
    beta_full = beta_rows.swapaxes(1, 2).reshape(width, count)
    beta_grad = lax.dynamic_slice_in_dim(beta_full, lax.axis_index("fsdp") * deep, deep, 0)
    return (
        dq[None], dk[None], dv[None], dhidden[None],
        down_grad, up_grad, beta_grad, bias_grad.reshape(-1), rate_grad.reshape(-1),
    )


def solution(mesh):
    shards, blocks_ctx = mesh.shape["fsdp"], mesh.shape["ctx"]
    tokens, state = P("fsdp", "ctx", None), P("fsdp", "ctx", None, None, None)
    by_row, by_col = P("fsdp", None), P(None, "fsdp")
    return jax.shard_map(
        functools.partial(on_device, shards, blocks_ctx),
        mesh=mesh,
        in_specs=(tokens,) * 5 + (state, by_row, by_col, P(), P(), by_row),
        out_specs=(tokens,) * 4 + (by_row, by_col, by_row, P(), P()),
        check_vma=False,
    )
```
